32 devices in a mesh: dom: 2 (over y), row: 4 (over z), aux: 2 (over x), sub: 2 (over core).
Axes of the slice: x: 2, y: 2, z: 4, core: 2. Of those that a mesh axis runs over, the one named last changes fastest.
Arguments:
- factor: float32 [512, 32, 256], P(('dom', 'row'), 'aux', 'sub'), parts along dimension 0, may hold values from -2 to 2
- density: float32 [512, 256], P(('dom', 'row')), parts along dimension 0, as said below
- screen: int32 [8, 4], P(('dom', 'row'), 'sub'), parts along dimension 0, may hold values from 0 to 3, as said below
Outputs:
- fock_exchange: float32 [512, 256], P(('dom', 'row'), ('aux', 'sub')), parts along dimension 0
The draws below stay inside these ranges and needn't reach their ends.
There are 2 independent parts, one for each index of `dom`. The reference program is written for one: setup_inputs(seed, part) draws one part's arguments, and reference() takes and returns one part's arrays. A program takes and returns all parts, laid end to end along the dimension named above; each array names one. Nothing has to cross between parts.
Inputs may be any that keep to these rules, and one draw needn't show every extreme that they name: `screen`: row I lists 4 distinct block indices, the first being I itself. density is exactly symmetric.
All inputs are finite; a program needn't handle non-finite values.
Results may differ from the reference program's by a relative error of at most 0.0003.
Values sent between devices are 32-bit elements; how exact they have to be, the bound alone decides.
No kernel may reach another device: no remote copies, remote signals or barrier semaphores. Data moves between devices by JAX's collectives and lax.ppermute only.
A program may use at most 128 MiB of HBM per device.

```python
import jax
import jax.numpy as jnp
from jax import lax

BLOCK = 64
SCREENED = 4
BLOCKS = 4
ORBITALS = 256
AUX = 32


def draw_density(key, part):
    raw = jax.random.normal(key, (ORBITALS, ORBITALS), jnp.float32)
    return (raw + raw.T) * (0.5 / ORBITALS ** 0.5)


def draw_screen(key, part):
    row_keys = jax.random.split(key, BLOCKS)

    def row_pick(row_key, row_index):
        others = jax.random.permutation(row_key, BLOCKS - 1)[:SCREENED - 1].astype(jnp.int32)
        others = others + (others >= row_index).astype(jnp.int32)
        return jnp.concatenate([row_index[None], others]).astype(jnp.int32)
    return jax.vmap(row_pick)(row_keys, jnp.arange(BLOCKS, dtype=jnp.int32))


def levels(stream_key, dims, cuts, low, largest):
    factor_of, own = 1.0, jax.random.fold_in(stream_key, 6)
    for dim, shards_of in cuts:
        steps = jnp.exp(jax.random.uniform(jax.random.fold_in(own, dim), (shards_of,), jnp.float32, low / len(cuts), largest / len(cuts)))
        factor_of = factor_of * jnp.repeat(steps, dims[dim] // shards_of).reshape([-1 if axis == dim else 1 for axis in range(len(dims))])
    return factor_of


def centred(stream_key, shape, spread, bound, pieces=(), kind=jnp.bfloat16):
    drawn = spread * jax.random.normal(stream_key, shape, jnp.float32)
    if pieces:
        drawn = drawn * levels(stream_key, shape, pieces, -0.22, 0.18)
    return jnp.clip(drawn, -bound, bound).astype(kind)


def setup_inputs(seed: int = 0, part: int = 0) -> dict:
    arg_keys = jax.random.split(jax.random.key(seed), 4)
    own_keys = jax.random.split(jax.random.fold_in(arg_keys[3], part), 4)
    return {
        "factor": centred(own_keys[0], (ORBITALS, AUX, SCREENED * BLOCK), (1.414 * (AUX * SCREENED * BLOCK) ** -0.25), 2.0, ((0, 4), (1, 2), (2, 2)), jnp.float32),
        "density": draw_density(jax.random.fold_in(jax.random.fold_in(arg_keys[3], part), 71), part),
        "screen": draw_screen(jax.random.fold_in(jax.random.fold_in(arg_keys[3], part), 71), part),
    }


precise = lax.Precision.HIGHEST


def reference(factor, density, screen):
    stacked = density.reshape(BLOCKS, BLOCK, ORBITALS)
    rows_all = factor.reshape(BLOCKS, BLOCK, AUX, SCREENED, BLOCK)

    def row_block(member):
        rows_one, screen_one = member
        panel = jnp.take(stacked, screen_one.astype(jnp.int32), axis=0).reshape(SCREENED * BLOCK, ORBITALS)
        contracted = jnp.einsum("ipk,kl->ipl", rows_one.reshape(BLOCK, AUX, SCREENED * BLOCK), panel,
                                precision=precise, preferred_element_type=jnp.float32)
        tiled = contracted.reshape(BLOCK, AUX, BLOCKS, BLOCK)
        picked = jnp.take(tiled, screen.astype(jnp.int32), axis=2)
        return jnp.einsum("ipnsl,njpsl->inj", picked, rows_all, precision=precise,
                          preferred_element_type=jnp.float32)

    result = lax.map(row_block, (rows_all, screen))
    return result.reshape(ORBITALS, ORBITALS)
```

```python
import functools

import jax
import jax.numpy as jnp
from jax import lax
from jax.experimental import pallas as pl
from jax.experimental.pallas import tpu as pltpu
from jax.sharding import PartitionSpec as P

precise = lax.Precision.HIGHEST
VMEM = pl.BlockSpec(memory_space=pltpu.VMEM)
SMEM = pl.BlockSpec(memory_space=pltpu.SMEM)
F32 = jnp.float32
BF16 = jnp.bfloat16


def call(kernel, outs, scratch=(), ins=None, count=0):
    return pl.pallas_call(
        kernel,
        out_shape=tuple(jax.ShapeDtypeStruct(s, F32) for s in outs),
        in_specs=ins if ins is not None else [VMEM] * count,
        out_specs=tuple(VMEM for _ in outs),
        scratch_shapes=list(scratch),
        compiler_params=pltpu.CompilerParams(vmem_limit_bytes=12 * 1024 * 1024),
    )


def swap(x, axes, size, k):
    return lax.ppermute(x, axes, [(a, a ^ k) for a in range(size)])


def split(x):
    high = x.astype(BF16)
    return high, (x - high.astype(F32)).astype(BF16)


def pack_kernel(aux_local, share, screen_ref, other_ref, own_ref, par_ref, *outs):
    r, s = lax.axis_index("row"), lax.axis_index("sub")
    size = own_ref.shape[0] // aux_local
    low = lax.broadcasted_iota(jnp.int32, (size, 128), 1) < 64
    half = jnp.where(low, 0, 1)
    places = []
    for ref in (screen_ref, other_ref):
        a, b = ref[0, 0], ref[0, 1]
        places += [jnp.where(low, a, b), jnp.where(low, b, a)]
    subs = 2
    for k, out in enumerate(outs):
        for j in range(share):
            p = ((r ^ k) * subs + s) * share + j
            v = own_ref[pl.ds(p, size, stride=aux_local), :]
            w = par_ref[pl.ds(p, size, stride=aux_local), :]
            parts = [v, pltpu.roll(v, 64, 1), w, pltpu.roll(w, 64, 1)]
            for h in range(out.shape[1] // 128):
                block = half + 2 * h
                value = jnp.zeros((size, 128), F32)
                for place, part in zip(places, parts):
                    value = jnp.where(place == block, part, value)
                out[j * size:(j + 1) * size, h * 128:(h + 1) * 128] = value


def fock_kernel(share, nrow, nquarter, *refs):
    chunks, refs = refs[:nrow], refs[nrow:]
    near, far, refs = refs[0], refs[1], refs[2:]
    outs, (dh, dl, bh, bl, total) = refs[:nquarter], refs[nquarter:]
    r = lax.axis_index("row")
    q = lax.axis_index("aux") * 2 + lax.axis_index("sub")
    size = chunks[0].shape[0] // share
    piece = near.shape[2]
    for dq in range(nquarter):
        for k in range(nrow):
            source = (near if dq % 2 == 0 else far)[dq // 2, k]
            start = pl.multiple_of((r ^ k) * size + (q ^ dq) * piece, piece)
            high, lower = split(source)
            dh[pl.ds(start, piece), :] = high
            dl[pl.ds(start, piece), :] = lower
    for k in range(nrow):
        start = pl.multiple_of((r ^ k) * size, size)
        for j in range(share):
            high, lower = split(chunks[k][j * size:(j + 1) * size, :])
            bh[j, pl.ds(start, size), :] = high
            bl[j, pl.ds(start, size), :] = lower
    dot = functools.partial(jnp.dot, preferred_element_type=F32)
    dot_t = lambda a, b: lax.dot_general(a, b, (((1,), (1,)), ((), ())), preferred_element_type=F32)
    result = None
    for j in range(share):
        b1, b2 = bh[j], bl[j]
        c = dot(b1, dh[...]) + (dot(b1, dl[...]) + dot(b2, dh[...]))
        c1, c2 = split(c)
        f = dot_t(c1, b1) + (dot_t(c1, b2) + dot_t(c2, b1))
        result = f if result is None else result + f
    total[...] = result
    for dq in range(nquarter):
        start = pl.multiple_of((q ^ dq) * size, size)
        outs[dq][...] = total[pl.ds(start, size), :]


def cut_kernel(nrow, *refs):
    ins, outs = refs[:-nrow], refs[-nrow:]
    r = lax.axis_index("row")
    value = ins[0][...] + ins[1][...] + (ins[2][...] + ins[3][...])
    size = value.shape[0]
    low = lax.broadcasted_iota(jnp.int32, (size // 2, 128), 1) < 64
    for k in range(nrow):
        block = r ^ k
        picked = value[:, :128]
        for h in range(1, value.shape[1] // 128):
            picked = jnp.where(block // 2 == h, value[:, h * 128:(h + 1) * 128], picked)
        turned = pltpu.roll(picked, 64, 1)
        odd = block % 2 == 1
        first = jnp.where(odd, turned, picked)[:size // 2]
        second = jnp.where(odd, picked, turned)[size // 2:]
        outs[k][...] = jnp.where(low, first, second)


def final_kernel(a, b, c, d, out):
    value = a[...] + b[...] + (c[...] + d[...])
    both = jnp.transpose(jnp.concatenate([value, pltpu.roll(value, 64, 1)], axis=0))
    size = out.shape[0]
    out[...] = both[:size, :]


def dealt_body(sizes, factor, density, screen):
    nrow, naux, nsub = sizes
    block_size, orbitals = density.shape
    aux_local = factor.shape[1]
    share = aux_local // (nrow * nsub)
    flat = factor.reshape(block_size * aux_local, factor.shape[2])
    other_screen = swap(screen, "sub", nsub, 1)
    other = swap(flat, "sub", nsub, 1)
    q = lax.axis_index("aux") * nsub + lax.axis_index("sub")
    nquarter = naux * nsub
    piece = block_size // nquarter
    quarter = lax.dynamic_slice_in_dim(density, q * piece, piece, 0)
    chunks = call(
        functools.partial(pack_kernel, aux_local, share),
        [(share * block_size, orbitals)] * nrow,
        ins=[SMEM, SMEM, VMEM, VMEM],
    )(screen, other_screen, flat, other)
    order = [3, 2, 1]
    moved = {k: swap(quarter, "row", nrow, k) for k in order}
    got = {k: swap(chunks[k], "row", nrow, k) for k in order}
    near = jnp.stack([quarter] + [moved[k] for k in range(1, nrow)])
    near = jnp.stack([near, swap(near, "aux", naux, 1)])
    far = swap(near, "sub", nsub, 1)
    parts = call(
        functools.partial(fock_kernel, share, nrow, nquarter),
        [(block_size, orbitals)] * nquarter,
        scratch=[
            pltpu.VMEM((orbitals, orbitals), BF16),
            pltpu.VMEM((orbitals, orbitals), BF16),
            pltpu.VMEM((share, orbitals, orbitals), BF16),
            pltpu.VMEM((share, orbitals, orbitals), BF16),
            pltpu.VMEM((orbitals, orbitals), F32),
        ],
        count=nrow + 2,
    )(chunks[0], *[got[k] for k in range(1, nrow)], near, far)
    sums = [parts[0]] + [swap(parts[k], ("aux", "sub"), nquarter, k) for k in range(1, nquarter)]
    cuts = call(
        functools.partial(cut_kernel, nrow), [(block_size // 2, 2 * block_size)] * nrow, count=nquarter
    )(*sums)
    last = [cuts[0]] + [swap(cuts[k], "row", nrow, k) for k in range(1, nrow)]
    return call(final_kernel, [(block_size, block_size)], count=nrow)(*last)[0]


def pair_block(tiled, block_rows, block_cols):
    block_size = tiled.shape[0]
    picked = jnp.take(tiled, block_cols, axis=2)
    others = block_rows.reshape(
        block_rows.shape[0], block_rows.shape[1], block_cols.shape[0], block_size
    )
    return jnp.einsum(
        "ipsl,jpsl->ij", picked, others, precision=precise, preferred_element_type=jnp.float32
    )


def gathered_body(factor, density, screen):
    block_size = density.shape[0]
    orbitals = density.shape[1]
    nblocks = orbitals // block_size
    aux_local = factor.shape[1]
    own_block = lax.axis_index("row")
    full_rows, full_screen = (
        lax.all_gather(factor, "sub", axis=2, tiled=True),
        lax.all_gather(screen, "sub", axis=1, tiled=True),
    )
    whole = lax.all_gather(density, "row", axis=0, tiled=True)
    stacked = whole.reshape(nblocks, block_size, orbitals)
    panel = jnp.take(stacked, screen[0], axis=0).reshape(-1, orbitals)
    contracted = jnp.einsum(
        "ipk,kl->ipl", factor, panel, precision=precise, preferred_element_type=jnp.float32
    )
    tiled = contracted.reshape(block_size, aux_local, nblocks, block_size)
    zero_block = jnp.zeros((block_size, block_size), jnp.float32)
    rows_piece = lax.all_gather(full_rows[None], "row", axis=0, tiled=True)
    screen_piece = lax.all_gather(full_screen, "row", axis=0, tiled=True)
    count = rows_piece.shape[0]

    def single(member):
        offset, rows_one, screen_one = member
        return lax.cond(
            offset >= own_block, lambda: pair_block(tiled, rows_one, screen_one), lambda: zero_block
        )

    computed = lax.map(single, (jnp.arange(count, dtype=jnp.int32), rows_piece, screen_piece))
    updated = jnp.transpose(computed, (1, 0, 2))
    keep_mask = (jnp.arange(nblocks, dtype=jnp.int32) != own_block).astype(jnp.float32)
    received = lax.all_to_all(updated, "row", split_axis=1, concat_axis=1, tiled=True)
    mirrored = jnp.transpose(received, (2, 1, 0)) * keep_mask[None, :, None]
    partial_value = (updated + mirrored).reshape(block_size, orbitals)
    return lax.psum_scatter(partial_value, ("aux", "sub"), scatter_dimension=1, tiled=True)


def solution(mesh):
    sizes = tuple(mesh.shape[a] for a in ("row", "aux", "sub"))

    def body(factor, density, screen):
        nrow, naux, nsub = sizes
        block_size, orbitals = density.shape
        fits = (
            naux * nsub == 4
            and nsub == 2
            and nrow == 4
            and block_size == 64
            and orbitals == nrow * block_size
            and factor.shape[2] == 128
            and factor.shape[1] % (nrow * nsub * 2) == 0
        )
        if fits:
            return dealt_body(sizes, factor, density, screen)
        return gathered_body(factor, density, screen)

    return jax.shard_map(
        body,
        mesh=mesh,
        in_specs=(
            P(("dom", "row"), "aux", "sub"),
            P(("dom", "row"), None),
            P(("dom", "row"), "sub"),
        ),
        out_specs=P(("dom", "row"), ("aux", "sub")),
        check_vma=False,
    )
```

```python
import functools

import jax
import jax.numpy as jnp
from jax import lax
from jax.experimental import pallas as pl
from jax.experimental.pallas import tpu as pltpu
from jax.sharding import PartitionSpec as P

precise = lax.Precision.HIGHEST
VMEM = pl.BlockSpec(memory_space=pltpu.VMEM)
SMEM = pl.BlockSpec(memory_space=pltpu.SMEM)
HBM = pl.BlockSpec(memory_space=pltpu.HBM)
FIRST = 54272 * 1024
F32 = jnp.float32
BF16 = jnp.bfloat16


def call(kernel, outs, scratch=(), ins=None, count=0, limit=12 << 20, alias={}):
    return pl.pallas_call(
        kernel,
        out_shape=tuple(jax.ShapeDtypeStruct(s, F32) for s in outs),
        in_specs=ins if ins is not None else [VMEM] * count,
        out_specs=tuple(VMEM for _ in outs),
        scratch_shapes=list(scratch),
        input_output_aliases=alias,
        compiler_params=pltpu.CompilerParams(vmem_limit_bytes=limit),
    )


def swap(x, axes, size, k):
    return lax.ppermute(x, axes, [(a, a ^ k) for a in range(size)])


def split(x):
    high = x.astype(BF16)
    return high, (x - high.astype(F32)).astype(BF16)


def lanes(ref, size):
    low = lax.broadcasted_iota(jnp.int32, (size, 128), 1) < 64
    a, b = ref[0, 0], ref[0, 1]
    return [jnp.where(low, a, b), jnp.where(low, b, a)]


def spread(places, part, start):
    size = part.shape[0]
    turned = pltpu.roll(part, 64, 1)
    half = jnp.where(lax.broadcasted_iota(jnp.int32, (size, 128), 1) < 64, 0, 1)
    columns = []
    for h, value in enumerate(start):
        value = jnp.where(places[0] == half + 2 * h, part, value)
        columns.append(jnp.where(places[1] == half + 2 * h, turned, value))
    return columns


def fold(block):
    size = block.shape[0]
    low = lax.broadcasted_iota(jnp.int32, (size // 2, 128), 1) < 64
    return jnp.where(low, block[:size // 2], pltpu.roll(block, 64, 1)[size // 2:])


def unfold(folded):
    return jnp.concatenate([folded, pltpu.roll(folded, 64, 1)], axis=0)


def column_block(value, b):
    picked = value[:, :128]
    for h in range(1, value.shape[1] // 128):
        picked = jnp.where(b // 2 == h, value[:, h * 128:(h + 1) * 128], picked)
    return jnp.where(b % 2 == 1, pltpu.roll(picked, 64, 1), picked)


def near_kernel(share, screen_hbm, own_hbm, density_hbm, *refs):
    outs, (screen_ref, own_ref, density_ref, sems) = refs[:4], refs[4:]
    r, s = lax.axis_index("row"), lax.axis_index("sub")
    size, orbitals = density_ref.shape
    aux_local = own_ref.shape[0] // size
    cut = orbitals // 128
    pairs = ((screen_hbm, screen_ref), (density_hbm, density_ref), (own_hbm, own_ref))
    copies = [pltpu.make_async_copy(a, b, sems.at[i]) for i, (a, b) in enumerate(pairs)]
    for copy in copies:
        copy.start()
    for copy in copies:
        copy.wait()
    places = lanes(screen_ref, size)
    for k, out in enumerate(outs):
        for j in range(share):
            p = ((r ^ k) * 2 + s) * share + j
            part = own_ref[pl.ds(p, size, stride=aux_local), :]
            start = [jnp.zeros((size, 128), F32)] * cut
            for h, value in enumerate(spread(places, part, start)):
                at = (j * cut + h) * size
                out[at:at + size, :] = value
    at = share * cut * size
    density = density_ref[...]
    for h in range(cut):
        outs[1][at + h * size:at + (h + 1) * size, :] = density[:, h * 128:(h + 1) * 128]
    corner = fold(column_block(density, r))
    outs[3][at:, :] = corner
    outs[2][at:at + size // 2, :] = corner
    outs[2][at + size // 2:, :] = fold(column_block(density, r ^ 1))


def far_kernel(share, size, screen_ref, par_ref, *refs):
    ins, outs = refs[:4], refs[4:]
    r, s = lax.axis_index("row"), lax.axis_index("sub")
    aux_local = par_ref.shape[0] // size
    places = lanes(screen_ref, size)
    cut = ins[0].shape[0] // (share * size)
    for k, (start, out) in enumerate(zip(ins, outs)):
        for j in range(share):
            p = ((r ^ k) * 2 + s) * share + j
            part = par_ref[pl.ds(p, size, stride=aux_local), :]
            spots = [slice((j * cut + h) * size, (j * cut + h + 1) * size) for h in range(cut)]
            for spot, value in zip(spots, spread(places, part, [start[x, :] for x in spots])):
                out[spot, :] = value
        at = share * cut * size
        if out.shape[0] > at:
            out[at:, :] = start[at:, :]


def fock_kernel(share, own, one, two, three, density, *refs):
    outs, (dense, dh, dl, bh, bl, total) = refs[:4], refs[4:]
    r, s = lax.axis_index("row"), lax.axis_index("sub")
    q = lax.axis_index("aux") * 2 + s
    size, orbitals = density.shape
    cut = orbitals // 128
    rows_of = lambda k: pl.ds(pl.multiple_of((r ^ k) * size, size), size)
    half = jnp.where(lax.broadcasted_iota(jnp.int32, (size, 128), 1) < 64, 0, 1)

    def complete(k, came):
        across = jnp.transpose(column_block(dense[...], r ^ k))[:size, :]
        came = [(column, unfold(block)) for column, block in came]
        came = [(column, jnp.where(half == 0, block, pltpu.roll(block, 64, 1))) for column, block in came]
        for h in range(cut):
            value = across[:, h * 128:(h + 1) * 128]
            for column, block in came:
                value = jnp.where(half + 2 * h == column, block, value)
            dense[rows_of(k), h * 128:(h + 1) * 128] = value

    dense[rows_of(0), :] = density[...]
    at = share * cut * size
    at = share * cut * size
    for h in range(cut):
        dense[rows_of(1), h * 128:(h + 1) * 128] = one[at + h * size:at + (h + 1) * size, :]
    complete(2, [(r ^ 2, two[at:at + size // 2, :]), (r ^ 3, two[at + size // 2:, :])])
    complete(3, [(r ^ 3, three[at:, :])])
    dh[...], dl[...] = split(dense[...])
    for k, chunk in enumerate((own, one, two, three)):
        for j in range(share):
            for h in range(cut):
                at = (j * cut + h) * size
                high, lower = split(chunk[at:at + size, :])
                bh[j, rows_of(k), h * 128:(h + 1) * 128] = high
                bl[j, rows_of(k), h * 128:(h + 1) * 128] = lower
    dot = functools.partial(jnp.dot, preferred_element_type=F32)
    dot_t = lambda a, b: lax.dot_general(a, b, (((1,), (1,)), ((), ())), preferred_element_type=F32)
    result = None
    for j in range(share):
        b1, b2 = bh[j], bl[j]
        c = dot(b1, dh[...]) + (dot(b1, dl[...]) + dot(b2, dh[...]))
        c1, c2 = split(c)
        f = dot_t(c1, b1) + (dot_t(c1, b2) + dot_t(c2, b1))
        result = f if result is None else result + f
    total[...] = result
    for dq in range(4):
        outs[dq][...] = total[pl.ds(pl.multiple_of((q ^ dq) * size, size), size), :]


def cut_kernel(*refs):
    ins, outs = refs[:4], refs[4:]
    r = lax.axis_index("row")
    value = ins[0][...] + ins[1][...] + (ins[2][...] + ins[3][...])
    for k in range(4):
        outs[k][...] = fold(column_block(value, r ^ k))


def final_kernel(a, b, c, d, out):
    value = a[...] + b[...] + (c[...] + d[...])
    out[...] = jnp.transpose(unfold(value))[:out.shape[0], :]


def dealt_body(factor, density, screen):
    block_size, orbitals = density.shape
    aux_local = factor.shape[1]
    share = aux_local // 8
    packed = share * orbitals // 128 * block_size
    flat = factor.reshape(block_size * aux_local, factor.shape[2])
    row = lambda x, k: swap(x, "row", 4, k)
    core = lambda x: swap(x, "sub", 2, 1)
    other = core(flat)
    shapes = [(packed + more, 128) for more in (0, orbitals // 2, block_size, block_size // 2)]
    sent = call(
        functools.partial(near_kernel, share),
        shapes,
        ins=[HBM] * 3,
        scratch=[
            pltpu.SMEM(screen.shape, jnp.int32),
            pltpu.VMEM(flat.shape, F32),
            pltpu.VMEM(density.shape, F32),
            pltpu.SemaphoreType.DMA((3,)),
        ],
        limit=FIRST,
    )(screen, flat, density)
    sent = call(
        functools.partial(far_kernel, share, block_size),
        shapes,
        ins=[SMEM] + [VMEM] * 5,
        alias={2 + k: k for k in range(4)},
    )(core(screen), other, *sent)
    three, two, one = [row(sent[k], k) for k in (3, 2, 1)]
    parts = call(
        functools.partial(fock_kernel, share),
        [(block_size, orbitals)] * 4,
        scratch=[
            pltpu.VMEM((orbitals, orbitals), F32),
            pltpu.VMEM((orbitals, orbitals), BF16),
            pltpu.VMEM((orbitals, orbitals), BF16),
            pltpu.VMEM((share, orbitals, orbitals), BF16),
            pltpu.VMEM((share, orbitals, orbitals), BF16),
            pltpu.VMEM((orbitals, orbitals), F32),
        ],
        count=5,
    )(sent[0], one, two, three, density)
    sums = [parts[0]] + [swap(parts[k], ("aux", "sub"), 4, k) for k in (1, 2, 3)]
    cuts = call(cut_kernel, [(block_size // 2, 2 * block_size)] * 4, count=4)(*sums)
    last = [cuts[0]] + [row(cuts[k], k) for k in (1, 2, 3)]
    return call(final_kernel, [(block_size, block_size)], count=4)(*last)[0]


def pair_block(tiled, block_rows, block_cols):
    block_size = tiled.shape[0]
    picked = jnp.take(tiled, block_cols, axis=2)
    others = block_rows.reshape(
        block_rows.shape[0], block_rows.shape[1], block_cols.shape[0], block_size
    )
    return jnp.einsum(
        "ipsl,jpsl->ij", picked, others, precision=precise, preferred_element_type=jnp.float32
    )


def gathered_body(factor, density, screen):
    block_size = density.shape[0]
    orbitals = density.shape[1]
    nblocks = orbitals // block_size
    aux_local = factor.shape[1]
    own_block = lax.axis_index("row")
    full_rows, full_screen = (
        lax.all_gather(factor, "sub", axis=2, tiled=True),
        lax.all_gather(screen, "sub", axis=1, tiled=True),
    )
    whole = lax.all_gather(density, "row", axis=0, tiled=True)
    stacked = whole.reshape(nblocks, block_size, orbitals)
    panel = jnp.take(stacked, screen[0], axis=0).reshape(-1, orbitals)
    contracted = jnp.einsum(
        "ipk,kl->ipl", factor, panel, precision=precise, preferred_element_type=jnp.float32
    )
    tiled = contracted.reshape(block_size, aux_local, nblocks, block_size)
    zero_block = jnp.zeros((block_size, block_size), jnp.float32)
    rows_piece = lax.all_gather(full_rows[None], "row", axis=0, tiled=True)
    screen_piece = lax.all_gather(full_screen, "row", axis=0, tiled=True)
    count = rows_piece.shape[0]

    def single(member):
        offset, rows_one, screen_one = member
        return lax.cond(
            offset >= own_block, lambda: pair_block(tiled, rows_one, screen_one), lambda: zero_block
        )

    computed = lax.map(single, (jnp.arange(count, dtype=jnp.int32), rows_piece, screen_piece))
    updated = jnp.transpose(computed, (1, 0, 2))
    keep_mask = (jnp.arange(nblocks, dtype=jnp.int32) != own_block).astype(jnp.float32)
    received = lax.all_to_all(updated, "row", split_axis=1, concat_axis=1, tiled=True)
    mirrored = jnp.transpose(received, (2, 1, 0)) * keep_mask[None, :, None]
    partial_value = (updated + mirrored).reshape(block_size, orbitals)
    return lax.psum_scatter(partial_value, ("aux", "sub"), scatter_dimension=1, tiled=True)


def solution(mesh):
    sizes = tuple(mesh.shape[a] for a in ("row", "aux", "sub"))

    def body(factor, density, screen):
        nrow, naux, nsub = sizes
        block_size, orbitals = density.shape
        fits = (
            naux * nsub == 4
            and nsub == 2
            and nrow == 4
            and block_size == 64
            and orbitals == nrow * block_size
            and factor.shape[2] == 128
            and factor.shape[1] % (nrow * nsub * 2) == 0
        )
        if fits:
            return dealt_body(factor, density, screen)
        return gathered_body(factor, density, screen)

    return jax.shard_map(
        body,
        mesh=mesh,
        in_specs=(
            P(("dom", "row"), "aux", "sub"),
            P(("dom", "row"), None),
            P(("dom", "row"), "sub"),
        ),
        out_specs=P(("dom", "row"), ("aux", "sub")),
        check_vma=False,
    )
```

```python
import functools

import jax
import jax.numpy as jnp
from jax import lax
from jax.experimental import pallas as pl
from jax.experimental.pallas import tpu as pltpu
from jax.sharding import PartitionSpec as P

precise = lax.Precision.HIGHEST
VMEM = pl.BlockSpec(memory_space=pltpu.VMEM)
HBM = pl.BlockSpec(memory_space=pltpu.HBM)
FIRST = 54272 * 1024
F32 = jnp.float32
BF16 = jnp.bfloat16


def call(kernel, outs, scratch=(), ins=None, count=0, limit=12 << 20, alias={}):
    return pl.pallas_call(
        kernel,
        out_shape=tuple(jax.ShapeDtypeStruct(s, F32) for s in outs),
        in_specs=ins if ins is not None else [VMEM] * count,
        out_specs=tuple(VMEM for _ in outs),
        scratch_shapes=list(scratch),
        input_output_aliases=alias,
        compiler_params=pltpu.CompilerParams(vmem_limit_bytes=limit),
    )


def swap(x, axes, size, k):
    return lax.ppermute(x, axes, [(a, a ^ k) for a in range(size)])


def split(x):
    high = x.astype(BF16)
    return high, (x - high.astype(F32)).astype(BF16)


def lanes(ref, size):
    low = lax.broadcasted_iota(jnp.int32, (size, 128), 1) < 64
    a, b = [jnp.broadcast_to(ref[0:1, i:i + 1], (size, 128)) for i in range(2)]
    return [jnp.where(low, a, b), jnp.where(low, b, a)]


def spread(places, part, start):
    size = part.shape[0]
    turned = pltpu.roll(part, 64, 1)
    half = jnp.where(lax.broadcasted_iota(jnp.int32, (size, 128), 1) < 64, 0, 1)
    columns = []
    for h, value in enumerate(start):
        value = jnp.where(places[0] == half + 2 * h, part, value)
        columns.append(jnp.where(places[1] == half + 2 * h, turned, value))
    return columns


def fold(block):
    size = block.shape[0]
    low = lax.broadcasted_iota(jnp.int32, (size // 2, 128), 1) < 64
    return jnp.where(low, block[:size // 2], pltpu.roll(block, 64, 1)[size // 2:])


def unfold(folded):
    return jnp.concatenate([folded, pltpu.roll(folded, 64, 1)], axis=0)


def half_of(value, h):
    return jnp.where(h == 0, value[:, :128], value[:, 128:])


def column_block(value, b):
    picked = half_of(value, b // 2)
    return jnp.where(b % 2 == 1, pltpu.roll(picked, 64, 1), picked)


def near_kernel(share, size, screen_hbm, own_hbm, *refs):
    outs, (screen_ref, own_ref, sems) = refs[:4], refs[4:]
    r, s = lax.axis_index("row"), lax.axis_index("sub")
    aux_local = own_ref.shape[0] // size
    cut = outs[0].shape[0] // (share * size)
    part_size = size // 2
    length = part_size * aux_local
    halves = [pl.ds(i * length, length) for i in range(2)]
    copies = [pltpu.make_async_copy(screen_hbm, screen_ref, sems.at[2])]
    copies += [pltpu.make_async_copy(own_hbm.at[x], own_ref.at[x], sems.at[i]) for i, x in enumerate(halves)]
    for copy in copies:
        copy.start()
    copies[0].wait()
    places = lanes(screen_ref, part_size)
    for i in range(2):
        copies[1 + i].wait()
        for k, out in enumerate(outs):
            for j in range(share):
                p = ((r ^ k) * 2 + s) * share + j + i * length
                part = own_ref[pl.ds(p, part_size, stride=aux_local), :]
                start = [jnp.zeros((part_size, 128), F32)] * cut
                for h, value in enumerate(spread(places, part, start)):
                    at = (j * cut + h) * size + i * part_size
                    out[at:at + part_size, :] = value


def far_kernel(share, screen_ref, par_ref, density_ref, *refs):
    ins, outs = refs[:4], refs[4:]
    r, s = lax.axis_index("row"), lax.axis_index("sub")
    size, orbitals = density_ref.shape
    aux_local = par_ref.shape[0] // size
    places = lanes(screen_ref, size)
    cut = orbitals // 128
    for k, (start, out) in enumerate(zip(ins, outs)):
        for j in range(share):
            p = ((r ^ k) * 2 + s) * share + j
            part = par_ref[pl.ds(p, size, stride=aux_local), :]
            spots = [slice((j * cut + h) * size, (j * cut + h + 1) * size) for h in range(cut)]
            for spot, value in zip(spots, spread(places, part, [start[x, :] for x in spots])):
                out[spot, :] = value
    at = share * cut * size
    density = density_ref[...]
    for h in range(cut):
        outs[1][at + h * size:at + (h + 1) * size, :] = density[:, h * 128:(h + 1) * 128]
    outs[2][at:, :] = half_of(density, r // 2)
    outs[3][at:, :] = fold(column_block(density, r))


def fock_kernel(share, own, one, two, three, density, *refs):
    outs, (dh, dl, bh, bl, total) = refs[:4], refs[4:]
    r = lax.axis_index("row")
    q = lax.axis_index("aux") * 2 + lax.axis_index("sub")
    size, orbitals = density.shape
    cut = orbitals // 128
    h, odd = r // 2, r % 2 == 1
    rows_of = lambda k: pl.ds(pl.multiple_of((r ^ k) * size, size), size)
    at = share * cut * size

    def keep(k, left, right):
        for x, value in enumerate((left, right)):
            high, lower = split(value)
            dh[rows_of(k), x * 128:(x + 1) * 128] = high
            dl[rows_of(k), x * 128:(x + 1) * 128] = lower

    mine = [density[:, x * 128:(x + 1) * 128] for x in range(2)]
    beside = [one[at + x * size:at + (x + 1) * size, :] for x in range(2)]
    keep(0, *mine)
    keep(1, *beside)
    a, b = [jnp.where(h == 0, x[1], x[0]) for x in (mine, beside)]
    across = jnp.transpose(jnp.concatenate([jnp.where(odd, b, a), jnp.where(odd, a, b)], axis=0))
    here = two[at:at + size, :]
    mirror = jnp.transpose(jnp.concatenate([here, here], axis=0))
    mirror = jnp.where(odd, mirror[:size], mirror[size:])
    corner = unfold(three[at:, :])
    corner = jnp.where(odd, corner, pltpu.roll(corner, 64, 1))
    low = lax.broadcasted_iota(jnp.int32, (size, 128), 1) < 64
    last = jnp.where(low ^ odd, mirror, corner)
    for k, inner, outer in (
        (2, here, jnp.where(odd, across[size:], across[:size])),
        (3, last, jnp.where(odd, across[:size], across[size:])),
    ):
        keep(k, jnp.where(h == 0, outer, inner), jnp.where(h == 0, inner, outer))
    for k, chunk in enumerate((own, one, two, three)):
        for j in range(share):
            for x in range(cut):
                at = (j * cut + x) * size
                high, lower = split(chunk[at:at + size, :])
                bh[j, rows_of(k), x * 128:(x + 1) * 128] = high
                bl[j, rows_of(k), x * 128:(x + 1) * 128] = lower
    dot = functools.partial(jnp.dot, preferred_element_type=F32)
    dot_t = lambda a, b: lax.dot_general(a, b, (((1,), (1,)), ((), ())), preferred_element_type=F32)
    result = None
    for j in range(share):
        b1, b2 = bh[j], bl[j]
        c = dot(b1, dh[...]) + (dot(b1, dl[...]) + dot(b2, dh[...]))
        c1, c2 = split(c)
        f = dot_t(c1, b1) + (dot_t(c1, b2) + dot_t(c2, b1))
        result = f if result is None else result + f
    total[...] = result
    for dq in range(4):
        outs[dq][...] = total[pl.ds(pl.multiple_of((q ^ dq) * size, size), size), :]


def cut_kernel(*refs):
    ins, outs = refs[:4], refs[4:]
    r = lax.axis_index("row")
    value = ins[0][...] + ins[1][...] + (ins[2][...] + ins[3][...])
    half = value.shape[0] // 2
    for k in range(4):
        outs[k % 2][k // 2 * half:(k // 2 + 1) * half, :] = fold(column_block(value, r ^ k))


def merge_kernel(kept, came, out, away):
    value = kept[...] + came[...]
    half = out.shape[0]
    out[...] = value[:half]
    away[...] = value[half:]


def final_kernel(kept, came, out):
    out[...] = jnp.transpose(unfold(kept[...] + came[...]))[:out.shape[0], :]


def dealt_body(factor, density, screen):
    block_size, orbitals = density.shape
    aux_local = factor.shape[1]
    share = aux_local // 8
    packed = share * orbitals // 128 * block_size
    flat = factor.reshape(block_size * aux_local, factor.shape[2])
    row = lambda x, k: swap(x, "row", 4, k)
    core = lambda x: swap(x, "sub", 2, 1)
    other = core(flat)
    shapes = [(packed + more, 128) for more in (0, orbitals // 2, block_size, block_size // 2)]
    sent = call(
        functools.partial(near_kernel, share, block_size),
        shapes,
        ins=[HBM] * 2,
        scratch=[
            pltpu.VMEM(screen.shape, jnp.int32),
            pltpu.VMEM(flat.shape, F32),
            pltpu.SemaphoreType.DMA((3,)),
        ],
        limit=FIRST,
    )(screen, flat)
    sent = call(
        functools.partial(far_kernel, share),
        shapes,
        count=7,
        alias={3 + k: k for k in range(4)},
    )(core(screen), other, density, *sent)
    three, two, one = [row(sent[k], k) for k in (3, 2, 1)]
    parts = call(
        functools.partial(fock_kernel, share),
        [(block_size, orbitals)] * 4,
        scratch=[
            pltpu.VMEM((orbitals, orbitals), BF16),
            pltpu.VMEM((orbitals, orbitals), BF16),
            pltpu.VMEM((share, orbitals, orbitals), BF16),
            pltpu.VMEM((share, orbitals, orbitals), BF16),
            pltpu.VMEM((orbitals, orbitals), F32),
        ],
        count=5,
    )(sent[0], one, two, three, density)
    sums = [parts[0]] + [swap(parts[k], ("aux", "sub"), 4, k) for k in (1, 2, 3)]
    kept, away = call(cut_kernel, [(block_size, 2 * block_size)] * 2, count=4)(*sums)
    kept, away = call(merge_kernel, [(block_size // 2, 2 * block_size)] * 2, count=2)(kept, row(away, 1))
    return call(final_kernel, [(block_size, block_size)], count=2)(kept, row(away, 2))[0]


def pair_block(tiled, block_rows, block_cols):
    block_size = tiled.shape[0]
    picked = jnp.take(tiled, block_cols, axis=2)
    others = block_rows.reshape(
        block_rows.shape[0], block_rows.shape[1], block_cols.shape[0], block_size
    )
    return jnp.einsum(
        "ipsl,jpsl->ij", picked, others, precision=precise, preferred_element_type=jnp.float32
    )


def gathered_body(factor, density, screen):
    block_size = density.shape[0]
    orbitals = density.shape[1]
    nblocks = orbitals // block_size
    aux_local = factor.shape[1]
    own_block = lax.axis_index("row")
    full_rows, full_screen = (
        lax.all_gather(factor, "sub", axis=2, tiled=True),
        lax.all_gather(screen, "sub", axis=1, tiled=True),
    )
    whole = lax.all_gather(density, "row", axis=0, tiled=True)
    stacked = whole.reshape(nblocks, block_size, orbitals)
    panel = jnp.take(stacked, screen[0], axis=0).reshape(-1, orbitals)
    contracted = jnp.einsum(
        "ipk,kl->ipl", factor, panel, precision=precise, preferred_element_type=jnp.float32
    )
    tiled = contracted.reshape(block_size, aux_local, nblocks, block_size)
    zero_block = jnp.zeros((block_size, block_size), jnp.float32)
    rows_piece = lax.all_gather(full_rows[None], "row", axis=0, tiled=True)
    screen_piece = lax.all_gather(full_screen, "row", axis=0, tiled=True)
    count = rows_piece.shape[0]

    def single(member):
        offset, rows_one, screen_one = member
        return lax.cond(
            offset >= own_block, lambda: pair_block(tiled, rows_one, screen_one), lambda: zero_block
        )

    computed = lax.map(single, (jnp.arange(count, dtype=jnp.int32), rows_piece, screen_piece))
    updated = jnp.transpose(computed, (1, 0, 2))
    keep_mask = (jnp.arange(nblocks, dtype=jnp.int32) != own_block).astype(jnp.float32)
    received = lax.all_to_all(updated, "row", split_axis=1, concat_axis=1, tiled=True)
    mirrored = jnp.transpose(received, (2, 1, 0)) * keep_mask[None, :, None]
    partial_value = (updated + mirrored).reshape(block_size, orbitals)
    return lax.psum_scatter(partial_value, ("aux", "sub"), scatter_dimension=1, tiled=True)


def solution(mesh):
    sizes = tuple(mesh.shape[a] for a in ("row", "aux", "sub"))

    def body(factor, density, screen):
        nrow, naux, nsub = sizes
        block_size, orbitals = density.shape
        fits = (
            naux * nsub == 4
            and nsub == 2
            and nrow == 4
            and block_size == 64
            and orbitals == nrow * block_size
            and factor.shape[2] == 128
            and factor.shape[1] % (nrow * nsub * 2) == 0
        )
        if fits:
            return dealt_body(factor, density, screen)
        return gathered_body(factor, density, screen)

    return jax.shard_map(
        body,
        mesh=mesh,
        in_specs=(
            P(("dom", "row"), "aux", "sub"),
            P(("dom", "row"), None),
            P(("dom", "row"), "sub"),
        ),
        out_specs=P(("dom", "row"), ("aux", "sub")),
        check_vma=False,
    )
```

```python
import functools

import jax
import jax.numpy as jnp
from jax import lax
from jax.experimental import pallas as pl
from jax.experimental.pallas import tpu as pltpu
from jax.sharding import PartitionSpec as P

precise = lax.Precision.HIGHEST
VMEM = pl.BlockSpec(memory_space=pltpu.VMEM)
HBM = pl.BlockSpec(memory_space=pltpu.HBM)
FIRST = 54272 * 1024
F32 = jnp.float32
BF16 = jnp.bfloat16


def call(kernel, outs, scratch=(), ins=None, count=0, limit=12 << 20, alias={}):
    return pl.pallas_call(
        kernel,
        out_shape=tuple(jax.ShapeDtypeStruct(s, F32) for s in outs),
        in_specs=ins if ins is not None else [VMEM] * count,
        out_specs=tuple(VMEM for _ in outs),
        scratch_shapes=list(scratch),
        input_output_aliases=alias,
        compiler_params=pltpu.CompilerParams(vmem_limit_bytes=limit),
    )


def swap(x, axes, size, k):
    return lax.ppermute(x, axes, [(a, a ^ k) for a in range(size)])


def split(x):
    high = x.astype(BF16)
    return high, (x - high.astype(F32)).astype(BF16)


def lanes(ref, size):
    low = lax.broadcasted_iota(jnp.int32, (size, 128), 1) < 64
    a, b = [jnp.broadcast_to(ref[0:1, i:i + 1], (size, 128)) for i in range(2)]
    return [jnp.where(low, a, b), jnp.where(low, b, a)]


def spread(places, part, start):
    size = part.shape[0]
    turned = pltpu.roll(part, 64, 1)
    half = jnp.where(lax.broadcasted_iota(jnp.int32, (size, 128), 1) < 64, 0, 1)
    columns = []
    for h, value in enumerate(start):
        block = (half + 2 * h).astype(places[0].dtype)
        value = jnp.where(places[0] == block, part, value)
        columns.append(jnp.where(places[1] == block, turned, value))
    return columns


def fold(block):
    size = block.shape[0]
    low = lax.broadcasted_iota(jnp.int32, (size // 2, 128), 1) < 64
    return jnp.where(low, block[:size // 2], pltpu.roll(block, 64, 1)[size // 2:])


def unfold(folded):
    return jnp.concatenate([folded, pltpu.roll(folded, 64, 1)], axis=0)


def half_of(value, h):
    return jnp.where(h == 0, value[:, :128], value[:, 128:])


def column_block(value, b):
    picked = half_of(value, b // 2)
    return jnp.where(b % 2 == 1, pltpu.roll(picked, 64, 1), picked)


def near_kernel(share, size, screen_hbm, own_hbm, *refs):
    raw, outs, (screen_ref, own_ref, sems) = refs[0], refs[1:4], refs[4:]
    r, s = lax.axis_index("row"), lax.axis_index("sub")
    aux_local = own_ref.shape[0] // size
    cut = outs[0].shape[0] // (share * size)
    part_size = size // 2
    length = part_size * aux_local
    halves = [pl.ds(i * length, length) for i in range(2)]
    copies = [pltpu.make_async_copy(screen_hbm, screen_ref, sems.at[2])]
    copies += [pltpu.make_async_copy(own_hbm.at[x], own_ref.at[x], sems.at[i]) for i, x in enumerate(halves)]
    for copy in copies:
        copy.start()
    copies[0].wait()
    places = lanes(screen_ref, part_size)
    even = lax.broadcasted_iota(jnp.int32, (8, 128), 0) % 2 == 0
    raw[2 * share * size:, :] = jnp.where(even, places[0][:8], places[1][:8]).astype(F32)
    for i in range(2):
        copies[1 + i].wait()
        for d in range(2):
            for j in range(share):
                p = ((r ^ 2) * 2 + (s ^ d)) * share + j + i * length
                at = (d * share + j) * size + i * part_size
                raw[at:at + part_size, :] = own_ref[pl.ds(p, part_size, stride=aux_local), :]
        for k, out in zip((0, 1, 3), outs):
            for j in range(share):
                p = ((r ^ k) * 2 + s) * share + j + i * length
                part = own_ref[pl.ds(p, part_size, stride=aux_local), :]
                start = [jnp.zeros((part_size, 128), F32)] * cut
                for h, value in enumerate(spread(places, part, start)):
                    at = (j * cut + h) * size + i * part_size
                    out[at:at + part_size, :] = value


def far_kernel(share, screen_ref, par_ref, density_ref, *refs):
    ins, outs, corner = refs[:3], refs[3:6], refs[6]
    r, s = lax.axis_index("row"), lax.axis_index("sub")
    size, orbitals = density_ref.shape
    aux_local = par_ref.shape[0] // size
    places = lanes(screen_ref, size)
    cut = orbitals // 128
    for k, start, out in zip((0, 1, 3), ins, outs):
        for j in range(share):
            p = ((r ^ k) * 2 + s) * share + j
            part = par_ref[pl.ds(p, size, stride=aux_local), :]
            spots = [slice((j * cut + h) * size, (j * cut + h + 1) * size) for h in range(cut)]
            for spot, value in zip(spots, spread(places, part, [start[x, :] for x in spots])):
                out[spot, :] = value
    at = share * cut * size
    density = density_ref[...]
    for h in range(cut):
        outs[1][at + h * size:at + (h + 1) * size, :] = density[:, h * 128:(h + 1) * 128]
    outs[2][at:, :] = half_of(density, r // 2)
    corner[...] = fold(column_block(density, r))


def fock_kernel(share, own, one, two, two_other, three, corner2, density, *refs):
    outs, (dh, dl, bh, bl, total) = refs[:4], refs[4:]
    r = lax.axis_index("row")
    q = lax.axis_index("aux") * 2 + lax.axis_index("sub")
    size, orbitals = density.shape
    cut = orbitals // 128
    h, odd = r // 2, r % 2 == 1
    rows_of = lambda k: pl.ds(pl.multiple_of((r ^ k) * size, size), size)
    at = share * cut * size

    def keep(k, left, right):
        for x, value in enumerate((left, right)):
            high, lower = split(value)
            dh[rows_of(k), x * 128:(x + 1) * 128] = high
            dl[rows_of(k), x * 128:(x + 1) * 128] = lower

    mine = [density[:, x * 128:(x + 1) * 128] for x in range(2)]
    beside = [one[at + x * size:at + (x + 1) * size, :] for x in range(2)]
    keep(0, *mine)
    keep(1, *beside)
    a, b = [jnp.where(h == 0, x[1], x[0]) for x in (mine, beside)]
    across = jnp.transpose(jnp.concatenate([jnp.where(odd, b, a), jnp.where(odd, a, b)], axis=0))
    here = three[at:at + size, :]
    mirror = jnp.transpose(jnp.concatenate([here, here], axis=0))
    mirror = jnp.where(odd, mirror[size:], mirror[:size])
    corner = unfold(corner2[...])
    corner = jnp.where(odd, pltpu.roll(corner, 64, 1), corner)
    low = lax.broadcasted_iota(jnp.int32, (size, 128), 1) < 64
    last = jnp.where(low ^ odd, corner, mirror)
    for k, inner, outer in (
        (2, last, jnp.where(odd, across[size:], across[:size])),
        (3, here, jnp.where(odd, across[:size], across[size:])),
    ):
        keep(k, jnp.where(h == 0, outer, inner), jnp.where(h == 0, inner, outer))
    for k, chunk in ((0, own), (1, one), (3, three)):
        for j in range(share):
            for x in range(cut):
                at = (j * cut + x) * size
                high, lower = split(chunk[at:at + size, :])
                bh[j, rows_of(k), x * 128:(x + 1) * 128] = high
                bl[j, rows_of(k), x * 128:(x + 1) * 128] = lower
    at = 2 * share * size
    spots = [
        [jnp.broadcast_to(ref[at + i:at + i + 1, :], (size, 128)) for i in range(2)] for ref in (two, two_other)
    ]
    for j in range(share):
        values = [jnp.zeros((size, 128), F32)] * cut
        for d, ref in enumerate((two, two_other)):
            x = (d * share + j) * size
            values = spread(spots[d], ref[x:x + size, :], values)
        for x, value in enumerate(values):
            high, lower = split(value)
            bh[j, rows_of(2), x * 128:(x + 1) * 128] = high
            bl[j, rows_of(2), x * 128:(x + 1) * 128] = lower
    dot = functools.partial(jnp.dot, preferred_element_type=F32)
    dot_t = lambda a, b: lax.dot_general(a, b, (((1,), (1,)), ((), ())), preferred_element_type=F32)
    result = None
    for j in range(share):
        b1, b2 = bh[j], bl[j]
        c = dot(b1, dh[...]) + (dot(b1, dl[...]) + dot(b2, dh[...]))
        c1, c2 = split(c)
        f = dot_t(c1, b1) + (dot_t(c1, b2) + dot_t(c2, b1))
        result = f if result is None else result + f
    total[...] = result
    for dq in range(4):
        outs[dq][...] = total[pl.ds(pl.multiple_of((q ^ dq) * size, size), size), :]


def cut_kernel(*refs):
    ins, outs = refs[:4], refs[4:]
    r = lax.axis_index("row")
    value = ins[0][...] + ins[1][...] + (ins[2][...] + ins[3][...])
    for k in range(4):
        outs[k][:value.shape[0] // 2, :] = fold(column_block(value, r ^ k))


def final_kernel(kept, one, two, three, out):
    half = out.shape[0] // 2
    value = kept[...] + one[:half, :] + (two[:half, :] + three[:half, :])
    out[...] = jnp.transpose(unfold(value))[:out.shape[0], :]


def dealt_body(factor, density, screen):
    block_size, orbitals = density.shape
    aux_local = factor.shape[1]
    share = aux_local // 8
    packed = share * orbitals // 128 * block_size
    flat = factor.reshape(block_size * aux_local, factor.shape[2])
    row = lambda x, k: swap(x, "row", 4, k)
    core = lambda x: swap(x, "sub", 2, 1)
    other = core(flat)
    shapes = [(packed + more, 128) for more in (0, orbitals // 2, block_size)]
    raw, *sent = call(
        functools.partial(near_kernel, share, block_size),
        [(2 * share * block_size + 8, 128)] + shapes,
        ins=[HBM] * 2,
        scratch=[
            pltpu.VMEM(screen.shape, jnp.int32),
            pltpu.VMEM(flat.shape, F32),
            pltpu.SemaphoreType.DMA((3,)),
        ],
        limit=FIRST,
    )(screen, flat)
    two = row(raw, 2)
    own, one, three, corner = call(
        functools.partial(far_kernel, share),
        shapes + [(block_size // 2, 128)],
        count=6,
        alias={3 + k: k for k in range(3)},
    )(core(screen), other, density, *sent)
    three, one, corner = row(three, 3), row(one, 1), row(corner, 2)
    parts = call(
        functools.partial(fock_kernel, share),
        [(block_size, orbitals)] * 4,
        scratch=[
            pltpu.VMEM((orbitals, orbitals), BF16),
            pltpu.VMEM((orbitals, orbitals), BF16),
            pltpu.VMEM((share, orbitals, orbitals), BF16),
            pltpu.VMEM((share, orbitals, orbitals), BF16),
            pltpu.VMEM((orbitals, orbitals), F32),
        ],
        count=7,
    )(own, one, two, core(two), three, corner, density)
    sums = [parts[0]] + [swap(parts[k], ("aux", "sub"), 4, k) for k in (1, 2, 3)]
    cuts = call(cut_kernel, [(block_size // 2 + more, 2 * block_size) for more in (0, 0, 16, 8)], count=4)(*sums)
    moved = [row(cuts[k], k) for k in (1, 2, 3)]
    return call(final_kernel, [(block_size, block_size)], count=4)(cuts[0], *moved)[0]


def pair_block(tiled, block_rows, block_cols):
    block_size = tiled.shape[0]
    picked = jnp.take(tiled, block_cols, axis=2)
    others = block_rows.reshape(
        block_rows.shape[0], block_rows.shape[1], block_cols.shape[0], block_size
    )
    return jnp.einsum(
        "ipsl,jpsl->ij", picked, others, precision=precise, preferred_element_type=jnp.float32
    )


def gathered_body(factor, density, screen):
    block_size = density.shape[0]
    orbitals = density.shape[1]
    nblocks = orbitals // block_size
    aux_local = factor.shape[1]
    own_block = lax.axis_index("row")
    full_rows, full_screen = (
        lax.all_gather(factor, "sub", axis=2, tiled=True),
        lax.all_gather(screen, "sub", axis=1, tiled=True),
    )
    whole = lax.all_gather(density, "row", axis=0, tiled=True)
    stacked = whole.reshape(nblocks, block_size, orbitals)
    panel = jnp.take(stacked, screen[0], axis=0).reshape(-1, orbitals)
    contracted = jnp.einsum(
        "ipk,kl->ipl", factor, panel, precision=precise, preferred_element_type=jnp.float32
    )
    tiled = contracted.reshape(block_size, aux_local, nblocks, block_size)
    zero_block = jnp.zeros((block_size, block_size), jnp.float32)
    rows_piece = lax.all_gather(full_rows[None], "row", axis=0, tiled=True)
    screen_piece = lax.all_gather(full_screen, "row", axis=0, tiled=True)
    count = rows_piece.shape[0]

    def single(member):
        offset, rows_one, screen_one = member
        return lax.cond(
            offset >= own_block, lambda: pair_block(tiled, rows_one, screen_one), lambda: zero_block
        )

    computed = lax.map(single, (jnp.arange(count, dtype=jnp.int32), rows_piece, screen_piece))
    updated = jnp.transpose(computed, (1, 0, 2))
    keep_mask = (jnp.arange(nblocks, dtype=jnp.int32) != own_block).astype(jnp.float32)
    received = lax.all_to_all(updated, "row", split_axis=1, concat_axis=1, tiled=True)
    mirrored = jnp.transpose(received, (2, 1, 0)) * keep_mask[None, :, None]
    partial_value = (updated + mirrored).reshape(block_size, orbitals)
    return lax.psum_scatter(partial_value, ("aux", "sub"), scatter_dimension=1, tiled=True)


def solution(mesh):
    sizes = tuple(mesh.shape[a] for a in ("row", "aux", "sub"))

    def body(factor, density, screen):
        nrow, naux, nsub = sizes
        block_size, orbitals = density.shape
        fits = (
            naux * nsub == 4
            and nsub == 2
            and nrow == 4
            and block_size == 64
            and orbitals == nrow * block_size
            and factor.shape[2] == 128
            and factor.shape[1] % (nrow * nsub * 2) == 0
        )
        if fits:
            return dealt_body(factor, density, screen)
        return gathered_body(factor, density, screen)

    return jax.shard_map(
        body,
        mesh=mesh,
        in_specs=(
            P(("dom", "row"), "aux", "sub"),
            P(("dom", "row"), None),
            P(("dom", "row"), "sub"),
        ),
        out_specs=P(("dom", "row"), ("aux", "sub")),
        check_vma=False,
    )
```

```python
import functools

import jax
import jax.numpy as jnp
from jax import lax
from jax.experimental import pallas as pl
from jax.experimental.pallas import tpu as pltpu
from jax.sharding import PartitionSpec as P

precise = lax.Precision.HIGHEST
VMEM = pl.BlockSpec(memory_space=pltpu.VMEM)
HBM = pl.BlockSpec(memory_space=pltpu.HBM)
FIRST = 54272 * 1024
F32 = jnp.float32
BF16 = jnp.bfloat16


def call(kernel, outs, scratch=(), ins=None, count=0, limit=12 << 20):
    return pl.pallas_call(
        kernel,
        out_shape=tuple(jax.ShapeDtypeStruct(s, F32) for s in outs),
        in_specs=ins if ins is not None else [VMEM] * count,
        out_specs=tuple(VMEM for _ in outs),
        scratch_shapes=list(scratch),
        compiler_params=pltpu.CompilerParams(vmem_limit_bytes=limit),
    )


def swap(x, axes, size, k):
    return lax.ppermute(x, axes, [(a, a ^ k) for a in range(size)])


def split(x):
    high = x.astype(BF16)
    return high, (x - high.astype(F32)).astype(BF16)


def lanes(ref, size):
    low = lax.broadcasted_iota(jnp.int32, (size, 128), 1) < 64
    a, b = [jnp.broadcast_to(ref[0:1, i:i + 1], (size, 128)) for i in range(2)]
    return [jnp.where(low, a, b), jnp.where(low, b, a)]


def spread(places, part, start):
    size = part.shape[0]
    turned = pltpu.roll(part, 64, 1)
    half = jnp.where(lax.broadcasted_iota(jnp.int32, (size, 128), 1) < 64, 0, 1)
    columns = []
    for h, value in enumerate(start):
        block = (half + 2 * h).astype(places[0].dtype)
        value = jnp.where(places[0] == block, part, value)
        columns.append(jnp.where(places[1] == block, turned, value))
    return columns


def fold(block):
    size = block.shape[0]
    low = lax.broadcasted_iota(jnp.int32, (size // 2, 128), 1) < 64
    return jnp.where(low, block[:size // 2], pltpu.roll(block, 64, 1)[size // 2:])


def unfold(folded):
    return jnp.concatenate([folded, pltpu.roll(folded, 64, 1)], axis=0)


def half_of(value, h):
    return jnp.where(h == 0, value[:, :128], value[:, 128:])


def column_block(value, b):
    picked = half_of(value, b // 2)
    return jnp.where(b % 2 == 1, pltpu.roll(picked, 64, 1), picked)


def near_kernel(share, size, own_hbm, raw, own, sems):
    r, s = lax.axis_index("row"), lax.axis_index("sub")
    aux_local = own.shape[0] // size
    part_size = size // 2
    length = part_size * aux_local
    halves = [pl.ds(i * length, length) for i in range(2)]
    copies = [pltpu.make_async_copy(own_hbm.at[x], own.at[x], sems.at[i]) for i, x in enumerate(halves)]
    for copy in copies:
        copy.start()
    for i in range(2):
        copies[i].wait()
        for d in range(2):
            for j in range(share):
                p = ((r ^ 2) * 2 + (s ^ d)) * share + j + i * length
                at = (d * share + j) * size + i * part_size
                raw[at:at + part_size, :] = own[pl.ds(p, part_size, stride=aux_local), :]


def far_kernel(share, screen_ref, other_ref, own_ref, par_ref, density_ref, *outs):
    r, s = lax.axis_index("row"), lax.axis_index("sub")
    outs, extra = outs[:3], outs[3]
    size, orbitals = density_ref.shape
    aux_local = par_ref.shape[0] // size
    sources = [(lanes(places, size), part) for places, part in ((screen_ref, own_ref), (other_ref, par_ref))]
    cut = orbitals // 128
    for k, out in zip((0, 1, 3), outs):
        for j in range(share):
            p = ((r ^ k) * 2 + s) * share + j
            values = [jnp.zeros((size, 128), F32)] * cut
            for places, part in sources:
                values = spread(places, part[pl.ds(p, size, stride=aux_local), :], values)
            for h, value in enumerate(values):
                at = (j * cut + h) * size
                out[at:at + size, :] = value
    at = share * cut * size
    density = density_ref[...]
    for h in range(cut):
        outs[1][at + h * size:at + (h + 1) * size, :] = density[:, h * 128:(h + 1) * 128]
    outs[2][at:, :] = half_of(density, r // 2)
    at = size // 2
    extra[:at, :] = fold(column_block(density, r))
    places = sources[0][0] + sources[1][0]
    row = lax.broadcasted_iota(jnp.int32, (8, 128), 0) % 4
    value = places[3][:8]
    for i in range(3):
        value = jnp.where(row == i, places[i][:8], value)
    extra[at:, :] = value.astype(F32)


def fock_kernel(share, own, one, two, two_other, three, extra2, density, *refs):
    outs, (dh, dl, bh, bl, total) = refs[:4], refs[4:]
    r = lax.axis_index("row")
    q = lax.axis_index("aux") * 2 + lax.axis_index("sub")
    size, orbitals = density.shape
    cut = orbitals // 128
    h, odd = r // 2, r % 2 == 1
    rows_of = lambda k: pl.ds(pl.multiple_of((r ^ k) * size, size), size)
    at = share * cut * size

    def keep(k, left, right):
        for x, value in enumerate((left, right)):
            high, lower = split(value)
            dh[rows_of(k), x * 128:(x + 1) * 128] = high
            dl[rows_of(k), x * 128:(x + 1) * 128] = lower

    mine = [density[:, x * 128:(x + 1) * 128] for x in range(2)]
    beside = [one[at + x * size:at + (x + 1) * size, :] for x in range(2)]
    keep(0, *mine)
    keep(1, *beside)
    a, b = [jnp.where(h == 0, x[1], x[0]) for x in (mine, beside)]
    across = jnp.transpose(jnp.concatenate([jnp.where(odd, b, a), jnp.where(odd, a, b)], axis=0))
    here = three[at:at + size, :]
    mirror = jnp.transpose(jnp.concatenate([here, here], axis=0))
    mirror = jnp.where(odd, mirror[size:], mirror[:size])
    corner = unfold(extra2[:size // 2, :])
    corner = jnp.where(odd, pltpu.roll(corner, 64, 1), corner)
    low = lax.broadcasted_iota(jnp.int32, (size, 128), 1) < 64
    last = jnp.where(low ^ odd, corner, mirror)
    for k, inner, outer in (
        (2, last, jnp.where(odd, across[size:], across[:size])),
        (3, here, jnp.where(odd, across[:size], across[size:])),
    ):
        keep(k, jnp.where(h == 0, outer, inner), jnp.where(h == 0, inner, outer))
    for k, chunk in ((0, own), (1, one), (3, three)):
        for j in range(share):
            for x in range(cut):
                at = (j * cut + x) * size
                high, lower = split(chunk[at:at + size, :])
                bh[j, rows_of(k), x * 128:(x + 1) * 128] = high
                bl[j, rows_of(k), x * 128:(x + 1) * 128] = lower
    at = size // 2
    spots = [
        [jnp.broadcast_to(extra2[at + 2 * d + i:at + 2 * d + i + 1, :], (size, 128)) for i in range(2)]
        for d in range(2)
    ]
    for j in range(share):
        values = [jnp.zeros((size, 128), F32)] * cut
        for d, ref in enumerate((two, two_other)):
            x = (d * share + j) * size
            values = spread(spots[d], ref[x:x + size, :], values)
        for x, value in enumerate(values):
            high, lower = split(value)
            bh[j, rows_of(2), x * 128:(x + 1) * 128] = high
            bl[j, rows_of(2), x * 128:(x + 1) * 128] = lower
    dot = functools.partial(jnp.dot, preferred_element_type=F32)
    dot_t = lambda a, b: lax.dot_general(a, b, (((1,), (1,)), ((), ())), preferred_element_type=F32)
    result = None
    for j in range(share):
        b1, b2 = bh[j], bl[j]
        c = dot(b1, dh[...]) + (dot(b1, dl[...]) + dot(b2, dh[...]))
        c1, c2 = split(c)
        f = dot_t(c1, b1) + (dot_t(c1, b2) + dot_t(c2, b1))
        result = f if result is None else result + f
    total[...] = result
    for dq in range(4):
        outs[dq][...] = total[pl.ds(pl.multiple_of((q ^ dq) * size, size), size), :]


def cut_kernel(*refs):
    ins, outs = refs[:4], refs[4:]
    r = lax.axis_index("row")
    value = ins[0][...] + ins[1][...] + (ins[2][...] + ins[3][...])
    for k in range(4):
        outs[k][:value.shape[0] // 2, :] = fold(column_block(value, r ^ k))


def final_kernel(kept, one, two, three, out):
    half = out.shape[0] // 2
    value = kept[...] + one[:half, :] + (two[:half, :] + three[:half, :])
    out[...] = jnp.transpose(unfold(value))[:out.shape[0], :]


def dealt_body(factor, density, screen):
    block_size, orbitals = density.shape
    aux_local = factor.shape[1]
    share = aux_local // 8
    packed = share * orbitals // 128 * block_size
    flat = factor.reshape(block_size * aux_local, factor.shape[2])
    row = lambda x, k: swap(x, "row", 4, k)
    core = lambda x: swap(x, "sub", 2, 1)
    other = core(flat)
    raw, mine = call(
        functools.partial(near_kernel, share, block_size),
        [(2 * share * block_size, 128), flat.shape],
        ins=[HBM],
        scratch=[pltpu.SemaphoreType.DMA((2,))],
        limit=FIRST,
    )(flat)
    two = row(raw, 2)
    own, one, three, extra = call(
        functools.partial(far_kernel, share),
        [(packed + more, 128) for more in (0, orbitals // 2, block_size)] + [(block_size // 2 + 8, 128)],
        count=5,
    )(screen, core(screen), mine, other, density)
    three, one, extra = row(three, 3), row(one, 1), row(extra, 2)
    parts = call(
        functools.partial(fock_kernel, share),
        [(block_size, orbitals)] * 4,
        scratch=[
            pltpu.VMEM((orbitals, orbitals), BF16),
            pltpu.VMEM((orbitals, orbitals), BF16),
            pltpu.VMEM((share, orbitals, orbitals), BF16),
            pltpu.VMEM((share, orbitals, orbitals), BF16),
            pltpu.VMEM((orbitals, orbitals), F32),
        ],
        count=7,
    )(own, one, two, core(two), three, extra, density)
    sums = [parts[0]] + [swap(parts[k], ("aux", "sub"), 4, k) for k in (1, 2, 3)]
    cuts = call(cut_kernel, [(block_size // 2 + more, 2 * block_size) for more in (0, 0, 16, 8)], count=4)(*sums)
    moved = [row(cuts[k], k) for k in (1, 2, 3)]
    return call(final_kernel, [(block_size, block_size)], count=4)(cuts[0], *moved)[0]


def pair_block(tiled, block_rows, block_cols):
    block_size = tiled.shape[0]
    picked = jnp.take(tiled, block_cols, axis=2)
    others = block_rows.reshape(
        block_rows.shape[0], block_rows.shape[1], block_cols.shape[0], block_size
    )
    return jnp.einsum(
        "ipsl,jpsl->ij", picked, others, precision=precise, preferred_element_type=jnp.float32
    )


def gathered_body(factor, density, screen):
    block_size = density.shape[0]
    orbitals = density.shape[1]
    nblocks = orbitals // block_size
    aux_local = factor.shape[1]
    own_block = lax.axis_index("row")
    full_rows, full_screen = (
        lax.all_gather(factor, "sub", axis=2, tiled=True),
        lax.all_gather(screen, "sub", axis=1, tiled=True),
    )
    whole = lax.all_gather(density, "row", axis=0, tiled=True)
    stacked = whole.reshape(nblocks, block_size, orbitals)
    panel = jnp.take(stacked, screen[0], axis=0).reshape(-1, orbitals)
    contracted = jnp.einsum(
        "ipk,kl->ipl", factor, panel, precision=precise, preferred_element_type=jnp.float32
    )
    tiled = contracted.reshape(block_size, aux_local, nblocks, block_size)
    zero_block = jnp.zeros((block_size, block_size), jnp.float32)
    rows_piece = lax.all_gather(full_rows[None], "row", axis=0, tiled=True)
    screen_piece = lax.all_gather(full_screen, "row", axis=0, tiled=True)
    count = rows_piece.shape[0]

    def single(member):
        offset, rows_one, screen_one = member
        return lax.cond(
            offset >= own_block, lambda: pair_block(tiled, rows_one, screen_one), lambda: zero_block
        )

    computed = lax.map(single, (jnp.arange(count, dtype=jnp.int32), rows_piece, screen_piece))
    updated = jnp.transpose(computed, (1, 0, 2))
    keep_mask = (jnp.arange(nblocks, dtype=jnp.int32) != own_block).astype(jnp.float32)
    received = lax.all_to_all(updated, "row", split_axis=1, concat_axis=1, tiled=True)
    mirrored = jnp.transpose(received, (2, 1, 0)) * keep_mask[None, :, None]
    partial_value = (updated + mirrored).reshape(block_size, orbitals)
    return lax.psum_scatter(partial_value, ("aux", "sub"), scatter_dimension=1, tiled=True)


def solution(mesh):
    sizes = tuple(mesh.shape[a] for a in ("row", "aux", "sub"))

    def body(factor, density, screen):
        nrow, naux, nsub = sizes
        block_size, orbitals = density.shape
        fits = (
            naux * nsub == 4
            and nsub == 2
            and nrow == 4
            and block_size == 64
            and orbitals == nrow * block_size
            and factor.shape[2] == 128
            and factor.shape[1] % (nrow * nsub * 2) == 0
        )
        if fits:
            return dealt_body(factor, density, screen)
        return gathered_body(factor, density, screen)

    return jax.shard_map(
        body,
        mesh=mesh,
        in_specs=(
            P(("dom", "row"), "aux", "sub"),
            P(("dom", "row"), None),
            P(("dom", "row"), "sub"),
        ),
        out_specs=P(("dom", "row"), ("aux", "sub")),
        check_vma=False,
    )
```

```python
import functools

import jax
import jax.numpy as jnp
from jax import lax
from jax.experimental import pallas as pl
from jax.experimental.pallas import tpu as pltpu
from jax.sharding import PartitionSpec as P

precise = lax.Precision.HIGHEST
VMEM = pl.BlockSpec(memory_space=pltpu.VMEM)
HBM = pl.BlockSpec(memory_space=pltpu.HBM)
FIRST = 54272 * 1024
F32 = jnp.float32
BF16 = jnp.bfloat16


def call(kernel, outs, scratch=(), ins=None, count=0, limit=12 << 20):
    return pl.pallas_call(
        kernel,
        out_shape=tuple(jax.ShapeDtypeStruct(s, F32) for s in outs),
        in_specs=ins if ins is not None else [VMEM] * count,
        out_specs=tuple(VMEM for _ in outs),
        scratch_shapes=list(scratch),
        compiler_params=pltpu.CompilerParams(vmem_limit_bytes=limit),
    )


def swap(x, axes, size, k):
    return lax.ppermute(x, axes, [(a, a ^ k) for a in range(size)])


def split(x):
    high = x.astype(BF16)
    return high, (x - high.astype(F32)).astype(BF16)


def lanes(ref, size):
    low = lax.broadcasted_iota(jnp.int32, (size, 128), 1) < 64
    a, b = [jnp.broadcast_to(ref[0:1, i:i + 1], (size, 128)) for i in range(2)]
    return [jnp.where(low, a, b), jnp.where(low, b, a)]


def spread(places, part, start):
    size = part.shape[0]
    turned = pltpu.roll(part, 64, 1)
    half = jnp.where(lax.broadcasted_iota(jnp.int32, (size, 128), 1) < 64, 0, 1)
    columns = []
    for h, value in enumerate(start):
        block = (half + 2 * h).astype(places[0].dtype)
        value = jnp.where(places[0] == block, part, value)
        columns.append(jnp.where(places[1] == block, turned, value))
    return columns


def fold(block):
    size = block.shape[0]
    low = lax.broadcasted_iota(jnp.int32, (size // 2, 128), 1) < 64
    return jnp.where(low, block[:size // 2], pltpu.roll(block, 64, 1)[size // 2:])


def unfold(folded):
    return jnp.concatenate([folded, pltpu.roll(folded, 64, 1)], axis=0)


def half_of(value, h):
    return jnp.where(h == 0, value[:, :128], value[:, 128:])


def column_block(value, b):
    picked = half_of(value, b // 2)
    return jnp.where(b % 2 == 1, pltpu.roll(picked, 64, 1), picked)


def near_kernel(share, size, own_hbm, raw, own, sems):
    r, s = lax.axis_index("row"), lax.axis_index("sub")
    aux_local = own.shape[0] // size
    part_size = size // 2
    length = part_size * aux_local
    halves = [pl.ds(i * length, length) for i in range(2)]
    copies = [pltpu.make_async_copy(own_hbm.at[x], own.at[x], sems.at[i]) for i, x in enumerate(halves)]
    for copy in copies:
        copy.start()
    for i in range(2):
        copies[i].wait()
        for d in range(2):
            for j in range(share):
                p = ((r ^ 2) * 2 + (s ^ d)) * share + j + i * length
                at = (d * share + j) * size + i * part_size
                raw[at:at + part_size, :] = own[pl.ds(p, part_size, stride=aux_local), :]


def extend_kernel(raw, screen_ref, density_ref, out):
    r, s = lax.axis_index("row"), lax.axis_index("sub")
    at = raw.shape[0]
    out[:at, :] = raw[...]
    folded = fold(column_block(density_ref[...], r))
    rows = folded.shape[0] // 2
    out[at:at + rows, :] = jnp.where(s == 0, folded[:rows], folded[rows:])
    direct, turned = lanes(screen_ref, 8)
    even = lax.broadcasted_iota(jnp.int32, (8, 128), 0) % 2 == 0
    out[at + rows:, :] = jnp.where(even, direct, turned).astype(F32)


def far_kernel(share, screen_ref, other_ref, own_ref, par_ref, density_ref, *outs):
    r, s = lax.axis_index("row"), lax.axis_index("sub")
    size, orbitals = density_ref.shape
    aux_local = par_ref.shape[0] // size
    sources = [(lanes(places, size), part) for places, part in ((screen_ref, own_ref), (other_ref, par_ref))]
    cut = orbitals // 128
    for k, out in zip((0, 1, 3), outs):
        for j in range(share):
            p = ((r ^ k) * 2 + s) * share + j
            values = [jnp.zeros((size, 128), F32)] * cut
            for places, part in sources:
                values = spread(places, part[pl.ds(p, size, stride=aux_local), :], values)
            for h, value in enumerate(values):
                at = (j * cut + h) * size
                out[at:at + size, :] = value
    at = share * cut * size
    density = density_ref[...]
    for h in range(cut):
        outs[1][at + h * size:at + (h + 1) * size, :] = density[:, h * 128:(h + 1) * 128]
    outs[2][at:, :] = half_of(density, r // 2)


def fock_kernel(share, own, one, two, two_other, three, density, *refs):
    outs, (dh, dl, bh, bl, total) = refs[:4], refs[4:]
    r, s = lax.axis_index("row"), lax.axis_index("sub")
    q = lax.axis_index("aux") * 2 + s
    size, orbitals = density.shape
    cut = orbitals // 128
    h, odd = r // 2, r % 2 == 1
    rows_of = lambda k: pl.ds(pl.multiple_of((r ^ k) * size, size), size)
    at = share * cut * size

    def keep(k, left, right):
        for x, value in enumerate((left, right)):
            high, lower = split(value)
            dh[rows_of(k), x * 128:(x + 1) * 128] = high
            dl[rows_of(k), x * 128:(x + 1) * 128] = lower

    mine = [density[:, x * 128:(x + 1) * 128] for x in range(2)]
    beside = [one[at + x * size:at + (x + 1) * size, :] for x in range(2)]
    keep(0, *mine)
    keep(1, *beside)
    a, b = [jnp.where(h == 0, x[1], x[0]) for x in (mine, beside)]
    across = jnp.transpose(jnp.concatenate([jnp.where(odd, b, a), jnp.where(odd, a, b)], axis=0))
    here = three[at:at + size, :]
    mirror = jnp.transpose(jnp.concatenate([here, here], axis=0))
    mirror = jnp.where(odd, mirror[size:], mirror[:size])
    at = 2 * share * size
    a, b = [ref[at:at + size // 4, :] for ref in (two, two_other)]
    corner = unfold(jnp.concatenate([jnp.where(s == 0, a, b), jnp.where(s == 0, b, a)], axis=0))
    corner = jnp.where(odd, pltpu.roll(corner, 64, 1), corner)
    low = lax.broadcasted_iota(jnp.int32, (size, 128), 1) < 64
    last = jnp.where(low ^ odd, corner, mirror)
    for k, inner, outer in (
        (2, last, jnp.where(odd, across[size:], across[:size])),
        (3, here, jnp.where(odd, across[:size], across[size:])),
    ):
        keep(k, jnp.where(h == 0, outer, inner), jnp.where(h == 0, inner, outer))
    for k, chunk in ((0, own), (1, one), (3, three)):
        for j in range(share):
            for x in range(cut):
                at = (j * cut + x) * size
                high, lower = split(chunk[at:at + size, :])
                bh[j, rows_of(k), x * 128:(x + 1) * 128] = high
                bl[j, rows_of(k), x * 128:(x + 1) * 128] = lower
    at = 2 * share * size + size // 4
    spots = [
        [jnp.broadcast_to(ref[at + i:at + i + 1, :], (size, 128)) for i in range(2)] for ref in (two, two_other)
    ]
    for j in range(share):
        values = [jnp.zeros((size, 128), F32)] * cut
        for d, ref in enumerate((two, two_other)):
            x = (d * share + j) * size
            values = spread(spots[d], ref[x:x + size, :], values)
        for x, value in enumerate(values):
            high, lower = split(value)
            bh[j, rows_of(2), x * 128:(x + 1) * 128] = high
            bl[j, rows_of(2), x * 128:(x + 1) * 128] = lower
    side = lambda *parts: jnp.concatenate(parts, axis=1)
    whole = jnp.concatenate([dh[...], dl[...], dh[...]], axis=0)
    lefts, rights = [], []
    for j in range(share):
        b1, b2 = bh[j], bl[j]
        c1, c2 = split(jnp.dot(side(b1, b1, b2), whole, preferred_element_type=F32))
        lefts += [c1, c1, c2]
        rights += [b1, b2, b1]
    result = lax.dot_general(
        side(*lefts), side(*rights), (((1,), (1,)), ((), ())), preferred_element_type=F32
    )
    total[...] = result
    for dq in range(4):
        outs[dq][...] = total[pl.ds(pl.multiple_of((q ^ dq) * size, size), size), :]


def cut_kernel(*refs):
    ins, outs = refs[:4], refs[4:]
    r = lax.axis_index("row")
    value = ins[0][...] + ins[1][...] + (ins[2][...] + ins[3][...])
    for k in range(4):
        outs[k][:value.shape[0] // 2, :] = fold(column_block(value, r ^ k))


def final_kernel(kept, one, two, three, out):
    half = out.shape[0] // 2
    value = kept[...] + one[:half, :] + (two[:half, :] + three[:half, :])
    out[...] = jnp.transpose(unfold(value))[:out.shape[0], :]


def dealt_body(factor, density, screen):
    block_size, orbitals = density.shape
    aux_local = factor.shape[1]
    share = aux_local // 8
    packed = share * orbitals // 128 * block_size
    flat = factor.reshape(block_size * aux_local, factor.shape[2])
    row = lambda x, k: swap(x, "row", 4, k)
    core = lambda x: swap(x, "sub", 2, 1)
    other = core(flat)
    raw, mine = call(
        functools.partial(near_kernel, share, block_size),
        [(2 * share * block_size, 128), flat.shape],
        ins=[HBM],
        scratch=[pltpu.SemaphoreType.DMA((2,))],
        limit=FIRST,
    )(flat)
    extended = (raw.shape[0] + block_size // 4 + 8, 128)
    two = row(call(extend_kernel, [extended], count=3)(raw, screen, density)[0], 2)
    own, one, three = call(
        functools.partial(far_kernel, share),
        [(packed + more, 128) for more in (0, orbitals // 2, block_size)],
        count=5,
    )(screen, core(screen), mine, other, density)
    three, one = row(three, 3), row(one, 1)
    parts = call(
        functools.partial(fock_kernel, share),
        [(block_size, orbitals)] * 4,
        scratch=[
            pltpu.VMEM((orbitals, orbitals), BF16),
            pltpu.VMEM((orbitals, orbitals), BF16),
            pltpu.VMEM((share, orbitals, orbitals), BF16),
            pltpu.VMEM((share, orbitals, orbitals), BF16),
            pltpu.VMEM((orbitals, orbitals), F32),
        ],
        count=6,
    )(own, one, two, core(two), three, density)
    sums = [parts[0]] + [swap(parts[k], ("aux", "sub"), 4, k) for k in (1, 2, 3)]
    cuts = call(cut_kernel, [(block_size // 2 + more, 2 * block_size) for more in (0, 0, 8, 16)], count=4)(*sums)
    moved = [row(cuts[k], k) for k in (1, 2, 3)]
    return call(final_kernel, [(block_size, block_size)], count=4)(cuts[0], *moved)[0]


def pair_block(tiled, block_rows, block_cols):
    block_size = tiled.shape[0]
    picked = jnp.take(tiled, block_cols, axis=2)
    others = block_rows.reshape(
        block_rows.shape[0], block_rows.shape[1], block_cols.shape[0], block_size
    )
    return jnp.einsum(
        "ipsl,jpsl->ij", picked, others, precision=precise, preferred_element_type=jnp.float32
    )


def gathered_body(factor, density, screen):
    block_size = density.shape[0]
    orbitals = density.shape[1]
    nblocks = orbitals // block_size
    aux_local = factor.shape[1]
    own_block = lax.axis_index("row")
    full_rows, full_screen = (
        lax.all_gather(factor, "sub", axis=2, tiled=True),
        lax.all_gather(screen, "sub", axis=1, tiled=True),
    )
    whole = lax.all_gather(density, "row", axis=0, tiled=True)
    stacked = whole.reshape(nblocks, block_size, orbitals)
    panel = jnp.take(stacked, screen[0], axis=0).reshape(-1, orbitals)
    contracted = jnp.einsum(
        "ipk,kl->ipl", factor, panel, precision=precise, preferred_element_type=jnp.float32
    )
    tiled = contracted.reshape(block_size, aux_local, nblocks, block_size)
    zero_block = jnp.zeros((block_size, block_size), jnp.float32)
    rows_piece = lax.all_gather(full_rows[None], "row", axis=0, tiled=True)
    screen_piece = lax.all_gather(full_screen, "row", axis=0, tiled=True)
    count = rows_piece.shape[0]

    def single(member):
        offset, rows_one, screen_one = member
        return lax.cond(
            offset >= own_block, lambda: pair_block(tiled, rows_one, screen_one), lambda: zero_block
        )

    computed = lax.map(single, (jnp.arange(count, dtype=jnp.int32), rows_piece, screen_piece))
    updated = jnp.transpose(computed, (1, 0, 2))
    keep_mask = (jnp.arange(nblocks, dtype=jnp.int32) != own_block).astype(jnp.float32)
    received = lax.all_to_all(updated, "row", split_axis=1, concat_axis=1, tiled=True)
    mirrored = jnp.transpose(received, (2, 1, 0)) * keep_mask[None, :, None]
    partial_value = (updated + mirrored).reshape(block_size, orbitals)
    return lax.psum_scatter(partial_value, ("aux", "sub"), scatter_dimension=1, tiled=True)


def solution(mesh):
    sizes = tuple(mesh.shape[a] for a in ("row", "aux", "sub"))

    def body(factor, density, screen):
        nrow, naux, nsub = sizes
        block_size, orbitals = density.shape
        fits = (
            naux * nsub == 4
            and nsub == 2
            and nrow == 4
            and block_size == 64
            and orbitals == nrow * block_size
            and factor.shape[2] == 128
            and factor.shape[1] % (nrow * nsub * 2) == 0
        )
        if fits:
            return dealt_body(factor, density, screen)
        return gathered_body(factor, density, screen)

    return jax.shard_map(
        body,
        mesh=mesh,
        in_specs=(
            P(("dom", "row"), "aux", "sub"),
            P(("dom", "row"), None),
            P(("dom", "row"), "sub"),
        ),
        out_specs=P(("dom", "row"), ("aux", "sub")),
        check_vma=False,
    )
```

```python
import functools

import jax
import jax.numpy as jnp
from jax import lax
from jax.experimental import pallas as pl
from jax.experimental.pallas import tpu as pltpu
from jax.sharding import PartitionSpec as P

precise = lax.Precision.HIGHEST
VMEM = pl.BlockSpec(memory_space=pltpu.VMEM)
HBM = pl.BlockSpec(memory_space=pltpu.HBM)
FIRST = 54272 * 1024
F32 = jnp.float32
BF16 = jnp.bfloat16


def call(kernel, outs, scratch=(), ins=None, count=0, limit=12 << 20):
    return pl.pallas_call(
        kernel,
        out_shape=tuple(jax.ShapeDtypeStruct(s, F32) for s in outs),
        in_specs=ins if ins is not None else [VMEM] * count,
        out_specs=tuple(VMEM for _ in outs),
        scratch_shapes=list(scratch),
        compiler_params=pltpu.CompilerParams(vmem_limit_bytes=limit),
    )


def swap(x, axes, size, k):
    return lax.ppermute(x, axes, [(a, a ^ k) for a in range(size)])


def split(x):
    high = x.astype(BF16)
    return high, (x - high.astype(F32)).astype(BF16)


def lanes(ref, size):
    low = lax.broadcasted_iota(jnp.int32, (size, 128), 1) < 64
    a, b = [jnp.broadcast_to(ref[0:1, i:i + 1], (size, 128)) for i in range(2)]
    return [jnp.where(low, a, b), jnp.where(low, b, a)]


def spread(places, part, start):
    size = part.shape[0]
    turned = pltpu.roll(part, 64, 1)
    half = jnp.where(lax.broadcasted_iota(jnp.int32, (size, 128), 1) < 64, 0, 1)
    columns = []
    for h, value in enumerate(start):
        block = (half + 2 * h).astype(places[0].dtype)
        value = jnp.where(places[0] == block, part, value)
        columns.append(jnp.where(places[1] == block, turned, value))
    return columns


def fold(block):
    size = block.shape[0]
    low = lax.broadcasted_iota(jnp.int32, (size // 2, 128), 1) < 64
    return jnp.where(low, block[:size // 2], pltpu.roll(block, 64, 1)[size // 2:])


def unfold(folded):
    return jnp.concatenate([folded, pltpu.roll(folded, 64, 1)], axis=0)


def half_of(value, h):
    return jnp.where(h == 0, value[:, :128], value[:, 128:])


def column_block(value, b):
    picked = half_of(value, b // 2)
    return jnp.where(b % 2 == 1, pltpu.roll(picked, 64, 1), picked)


def near_kernel(share, size, own_hbm, raw, own, sems):
    r, s = lax.axis_index("row"), lax.axis_index("sub")
    aux_local = own.shape[0] // size
    part_size = size // 2
    length = part_size * aux_local
    halves = [pl.ds(i * length, length) for i in range(2)]
    copies = [pltpu.make_async_copy(own_hbm.at[x], own.at[x], sems.at[i]) for i, x in enumerate(halves)]
    for copy in copies:
        copy.start()
    for i in range(2):
        copies[i].wait()
        for d in range(2):
            for j in range(share):
                p = ((r ^ 2) * 2 + (s ^ d)) * share + j + i * length
                at = (d * share + j) * size + i * part_size
                raw[at:at + part_size, :] = own[pl.ds(p, part_size, stride=aux_local), :]


def extend_kernel(raw, other_ref, density_ref, out):
    r, s = lax.axis_index("row"), lax.axis_index("sub")
    at = raw.shape[0]
    out[:at, :] = raw[...]
    folded = fold(column_block(density_ref[...], r))
    rows = folded.shape[0] // 2
    out[at:at + rows, :] = jnp.where(s == 0, folded[:rows], folded[rows:])
    direct, turned = lanes(other_ref, 8)
    even = lax.broadcasted_iota(jnp.int32, (8, 128), 0) % 2 == 0
    out[at + rows:, :] = jnp.where(even, direct, turned).astype(F32)


def far_kernel(share, screen_ref, other_ref, own_ref, par_ref, density_ref, *outs):
    r, s = lax.axis_index("row"), lax.axis_index("sub")
    size, orbitals = density_ref.shape
    aux_local = par_ref.shape[0] // size
    sources = [(lanes(places, size), part) for places, part in ((screen_ref, own_ref), (other_ref, par_ref))]
    cut = orbitals // 128
    for k, out in zip((0, 1, 3), outs):
        for j in range(share):
            p = ((r ^ k) * 2 + s) * share + j
            values = [jnp.zeros((size, 128), F32)] * cut
            for places, part in sources:
                values = spread(places, part[pl.ds(p, size, stride=aux_local), :], values)
            for h, value in enumerate(values):
                at = (j * cut + h) * size
                out[at:at + size, :] = value
    at = share * cut * size
    density = density_ref[...]
    for h in range(cut):
        outs[1][at + h * size:at + (h + 1) * size, :] = density[:, h * 128:(h + 1) * 128]
    outs[2][at:, :] = half_of(density, r // 2)


def fock_kernel(share, own, one, two, two_other, three, density, *refs):
    outs, (dh, dl, bh, bl, total) = refs[:4], refs[4:]
    r, s = lax.axis_index("row"), lax.axis_index("sub")
    q = lax.axis_index("aux") * 2 + s
    size, orbitals = density.shape
    cut = orbitals // 128
    h, odd = r // 2, r % 2 == 1
    rows_of = lambda k: pl.ds(pl.multiple_of((r ^ k) * size, size), size)
    at = share * cut * size

    def keep(k, left, right):
        for x, value in enumerate((left, right)):
            high, lower = split(value)
            dh[rows_of(k), x * 128:(x + 1) * 128] = high
            dl[rows_of(k), x * 128:(x + 1) * 128] = lower

    mine = [density[:, x * 128:(x + 1) * 128] for x in range(2)]
    beside = [one[at + x * size:at + (x + 1) * size, :] for x in range(2)]
    keep(0, *mine)
    keep(1, *beside)
    a, b = [jnp.where(h == 0, x[1], x[0]) for x in (mine, beside)]
    across = jnp.transpose(jnp.concatenate([jnp.where(odd, b, a), jnp.where(odd, a, b)], axis=0))
    here = three[at:at + size, :]
    mirror = jnp.transpose(jnp.concatenate([here, here], axis=0))
    mirror = jnp.where(odd, mirror[size:], mirror[:size])
    at = 2 * share * size
    a, b = [ref[at:at + size // 4, :] for ref in (two, two_other)]
    corner = unfold(jnp.concatenate([jnp.where(s == 0, a, b), jnp.where(s == 0, b, a)], axis=0))
    corner = jnp.where(odd, pltpu.roll(corner, 64, 1), corner)
    low = lax.broadcasted_iota(jnp.int32, (size, 128), 1) < 64
    last = jnp.where(low ^ odd, corner, mirror)
    for k, inner, outer in (
        (2, last, jnp.where(odd, across[size:], across[:size])),
        (3, here, jnp.where(odd, across[:size], across[size:])),
    ):
        keep(k, jnp.where(h == 0, outer, inner), jnp.where(h == 0, inner, outer))
    for k, chunk in ((0, own), (1, one), (3, three)):
        for j in range(share):
            for x in range(cut):
                at = (j * cut + x) * size
                high, lower = split(chunk[at:at + size, :])
                bh[j, rows_of(k), x * 128:(x + 1) * 128] = high
                bl[j, rows_of(k), x * 128:(x + 1) * 128] = lower
    at = 2 * share * size + size // 4
    spots = [
        [jnp.broadcast_to(ref[at + i:at + i + 1, :], (size, 128)) for i in range(2)] for ref in (two_other, two)
    ]
    for j in range(share):
        values = [jnp.zeros((size, 128), F32)] * cut
        for d, ref in enumerate((two, two_other)):
            x = (d * share + j) * size
            values = spread(spots[d], ref[x:x + size, :], values)
        for x, value in enumerate(values):
            high, lower = split(value)
            bh[j, rows_of(2), x * 128:(x + 1) * 128] = high
            bl[j, rows_of(2), x * 128:(x + 1) * 128] = lower
    side = lambda *parts: jnp.concatenate(parts, axis=1)
    whole = jnp.concatenate([dh[...], dl[...], dh[...]], axis=0)
    lefts, rights = [], []
    for j in range(share):
        b1, b2 = bh[j], bl[j]
        c1, c2 = split(jnp.dot(side(b1, b1, b2), whole, preferred_element_type=F32))
        lefts += [c1, c1, c2]
        rights += [b1, b2, b1]
    result = lax.dot_general(
        side(*lefts), side(*rights), (((1,), (1,)), ((), ())), preferred_element_type=F32
    )
    total[...] = result
    for dq in range(4):
        outs[dq][...] = total[pl.ds(pl.multiple_of((q ^ dq) * size, size), size), :]


def cut_kernel(*refs):
    ins, outs = refs[:4], refs[4:]
    r = lax.axis_index("row")
    value = ins[0][...] + ins[1][...] + (ins[2][...] + ins[3][...])
    for k in range(4):
        outs[k][:value.shape[0] // 2, :] = fold(column_block(value, r ^ k))


def final_kernel(kept, one, two, three, out):
    half = out.shape[0] // 2
    value = kept[...] + one[:half, :] + (two[:half, :] + three[:half, :])
    out[...] = jnp.transpose(unfold(value))[:out.shape[0], :]


def dealt_body(factor, density, screen):
    block_size, orbitals = density.shape
    aux_local = factor.shape[1]
    share = aux_local // 8
    packed = share * orbitals // 128 * block_size
    flat = factor.reshape(block_size * aux_local, factor.shape[2])
    row = lambda x, k: swap(x, "row", 4, k)
    core = lambda x: swap(x, "sub", 2, 1)
    other = core(flat)
    raw, mine = call(
        functools.partial(near_kernel, share, block_size),
        [(2 * share * block_size, 128), flat.shape],
        ins=[HBM],
        scratch=[pltpu.SemaphoreType.DMA((2,))],
        limit=FIRST,
    )(flat)
    extended = (raw.shape[0] + block_size // 4 + 8, 128)
    other_screen = core(screen)
    two = row(call(extend_kernel, [extended], count=3)(raw, other_screen, density)[0], 2)
    own, one, three = call(
        functools.partial(far_kernel, share),
        [(packed + more, 128) for more in (0, orbitals // 2, block_size)],
        count=5,
    )(screen, other_screen, mine, other, density)
    three, one = row(three, 3), row(one, 1)
    parts = call(
        functools.partial(fock_kernel, share),
        [(block_size, orbitals)] * 4,
        scratch=[
            pltpu.VMEM((orbitals, orbitals), BF16),
            pltpu.VMEM((orbitals, orbitals), BF16),
            pltpu.VMEM((share, orbitals, orbitals), BF16),
            pltpu.VMEM((share, orbitals, orbitals), BF16),
            pltpu.VMEM((orbitals, orbitals), F32),
        ],
        count=6,
    )(own, one, two, core(two), three, density)
    sums = [parts[0]] + [swap(parts[k], ("aux", "sub"), 4, k) for k in (1, 2, 3)]
    cuts = call(cut_kernel, [(block_size // 2 + more, 2 * block_size) for more in (0, 0, 8, 16)], count=4)(*sums)
    moved = [row(cuts[k], k) for k in (1, 2, 3)]
    return call(final_kernel, [(block_size, block_size)], count=4)(cuts[0], *moved)[0]


def pair_block(tiled, block_rows, block_cols):
    block_size = tiled.shape[0]
    picked = jnp.take(tiled, block_cols, axis=2)
    others = block_rows.reshape(
        block_rows.shape[0], block_rows.shape[1], block_cols.shape[0], block_size
    )
    return jnp.einsum(
        "ipsl,jpsl->ij", picked, others, precision=precise, preferred_element_type=jnp.float32
    )


def gathered_body(factor, density, screen):
    block_size = density.shape[0]
    orbitals = density.shape[1]
    nblocks = orbitals // block_size
    aux_local = factor.shape[1]
    own_block = lax.axis_index("row")
    full_rows, full_screen = (
        lax.all_gather(factor, "sub", axis=2, tiled=True),
        lax.all_gather(screen, "sub", axis=1, tiled=True),
    )
    whole = lax.all_gather(density, "row", axis=0, tiled=True)
    stacked = whole.reshape(nblocks, block_size, orbitals)
    panel = jnp.take(stacked, screen[0], axis=0).reshape(-1, orbitals)
    contracted = jnp.einsum(
        "ipk,kl->ipl", factor, panel, precision=precise, preferred_element_type=jnp.float32
    )
    tiled = contracted.reshape(block_size, aux_local, nblocks, block_size)
    zero_block = jnp.zeros((block_size, block_size), jnp.float32)
    rows_piece = lax.all_gather(full_rows[None], "row", axis=0, tiled=True)
    screen_piece = lax.all_gather(full_screen, "row", axis=0, tiled=True)
    count = rows_piece.shape[0]

    def single(member):
        offset, rows_one, screen_one = member
        return lax.cond(
            offset >= own_block, lambda: pair_block(tiled, rows_one, screen_one), lambda: zero_block
        )

    computed = lax.map(single, (jnp.arange(count, dtype=jnp.int32), rows_piece, screen_piece))
    updated = jnp.transpose(computed, (1, 0, 2))
    keep_mask = (jnp.arange(nblocks, dtype=jnp.int32) != own_block).astype(jnp.float32)
    received = lax.all_to_all(updated, "row", split_axis=1, concat_axis=1, tiled=True)
    mirrored = jnp.transpose(received, (2, 1, 0)) * keep_mask[None, :, None]
    partial_value = (updated + mirrored).reshape(block_size, orbitals)
    return lax.psum_scatter(partial_value, ("aux", "sub"), scatter_dimension=1, tiled=True)


def solution(mesh):
    sizes = tuple(mesh.shape[a] for a in ("row", "aux", "sub"))

    def body(factor, density, screen):
        nrow, naux, nsub = sizes
        block_size, orbitals = density.shape
        fits = (
            naux * nsub == 4
            and nsub == 2
            and nrow == 4
            and block_size == 64
            and orbitals == nrow * block_size
            and factor.shape[2] == 128
            and factor.shape[1] % (nrow * nsub * 2) == 0
        )
        if fits:
            return dealt_body(factor, density, screen)
        return gathered_body(factor, density, screen)

    return jax.shard_map(
        body,
        mesh=mesh,
        in_specs=(
            P(("dom", "row"), "aux", "sub"),
            P(("dom", "row"), None),
            P(("dom", "row"), "sub"),
        ),
        out_specs=P(("dom", "row"), ("aux", "sub")),
        check_vma=False,
    )
```

```python
import functools

import jax
import jax.numpy as jnp
from jax import lax
from jax.experimental import pallas as pl
from jax.experimental.pallas import tpu as pltpu
from jax.sharding import PartitionSpec as P

precise = lax.Precision.HIGHEST
VMEM = pl.BlockSpec(memory_space=pltpu.VMEM)
HBM = pl.BlockSpec(memory_space=pltpu.HBM)
FIRST = 54272 * 1024
F32 = jnp.float32
BF16 = jnp.bfloat16


def call(kernel, outs, scratch=(), ins=None, count=0, limit=12 << 20):
    return pl.pallas_call(
        kernel,
        out_shape=tuple(jax.ShapeDtypeStruct(s, F32) for s in outs),
        in_specs=ins if ins is not None else [VMEM] * count,
        out_specs=tuple(VMEM for _ in outs),
        scratch_shapes=list(scratch),
        compiler_params=pltpu.CompilerParams(vmem_limit_bytes=limit),
    )


def swap(x, axes, size, k):
    return lax.ppermute(x, axes, [(a, a ^ k) for a in range(size)])


def split(x):
    high = x.astype(BF16)
    return high, (x - high.astype(F32)).astype(BF16)


def lanes(ref, size):
    low = lax.broadcasted_iota(jnp.int32, (size, 128), 1) < 64
    a, b = [jnp.broadcast_to(ref[0:1, i:i + 1], (size, 128)) for i in range(2)]
    return [jnp.where(low, a, b), jnp.where(low, b, a)]


def spread(places, part, start):
    size = part.shape[0]
    turned = pltpu.roll(part, 64, 1)
    half = jnp.where(lax.broadcasted_iota(jnp.int32, (size, 128), 1) < 64, 0, 1)
    columns = []
    for h, value in enumerate(start):
        block = (half + 2 * h).astype(places[0].dtype)
        value = jnp.where(places[0] == block, part, value)
        columns.append(jnp.where(places[1] == block, turned, value))
    return columns


def fold(block):
    size = block.shape[0]
    low = lax.broadcasted_iota(jnp.int32, (size // 2, 128), 1) < 64
    return jnp.where(low, block[:size // 2], pltpu.roll(block, 64, 1)[size // 2:])


def unfold(folded):
    return jnp.concatenate([folded, pltpu.roll(folded, 64, 1)], axis=0)


def half_of(value, h):
    return jnp.where(h == 0, value[:, :128], value[:, 128:])


def column_block(value, b):
    picked = half_of(value, b // 2)
    return jnp.where(b % 2 == 1, pltpu.roll(picked, 64, 1), picked)


def near_kernel(share, size, own_hbm, raw, own, sems):
    r, s = lax.axis_index("row"), lax.axis_index("sub")
    aux_local = own.shape[0] // size
    part_size = size // 2
    length = part_size * aux_local
    halves = [pl.ds(i * length, length) for i in range(2)]
    copies = [pltpu.make_async_copy(own_hbm.at[x], own.at[x], sems.at[i]) for i, x in enumerate(halves)]
    for copy in copies:
        copy.start()
    for i in range(2):
        copies[i].wait()
        for d in range(2):
            for j in range(share):
                p = ((r ^ 2) * 2 + (s ^ d)) * share + j + i * length
                at = ((1 - d) * share + j) * size + i * part_size
                raw[at:at + part_size, :] = own[pl.ds(p, part_size, stride=aux_local), :]


def extend_kernel(raw, other_ref, density_ref, out):
    r, s = lax.axis_index("row"), lax.axis_index("sub")
    at, rows = raw.shape[0] // 2, density_ref.shape[0] // 2
    out[:at, :] = raw[:at, :]
    some = pl.ds(pl.multiple_of(s * rows, rows), rows)
    out[at:at + rows, :] = half_of(density_ref[some, :], r // 2)
    direct, turned = lanes(other_ref, 8)
    even = lax.broadcasted_iota(jnp.int32, (8, 128), 0) % 2 == 0
    out[at + rows:at + rows + 8, :] = jnp.where(even, direct, turned).astype(F32)
    out[at + rows + 8:, :] = raw[at:, :]


def pass_kernel(two, out):
    out[...] = two[:out.shape[0], :]


def far_kernel(share, screen_ref, other_ref, own_ref, par_ref, density_ref, *outs):
    r, s = lax.axis_index("row"), lax.axis_index("sub")
    size, orbitals = density_ref.shape
    aux_local = par_ref.shape[0] // size
    sources = [(lanes(places, size), part) for places, part in ((screen_ref, own_ref), (other_ref, par_ref))]
    cut = orbitals // 128
    for k, out in zip((0, 1, 3), outs):
        for j in range(share):
            p = ((r ^ k) * 2 + s) * share + j
            values = [jnp.zeros((size, 128), F32)] * cut
            for places, part in sources:
                values = spread(places, part[pl.ds(p, size, stride=aux_local), :], values)
            for h, value in enumerate(values):
                at = (j * cut + h) * size
                out[at:at + size, :] = value
    at = share * cut * size
    density = density_ref[...]
    for h in range(cut):
        outs[1][at + h * size:at + (h + 1) * size, :] = density[:, h * 128:(h + 1) * 128]
    outs[2][at:, :] = fold(column_block(density, r))


def fock_kernel(share, own, one, two, two_other, three, density, *refs):
    outs, (dh, dl, bh, bl, total) = refs[:4], refs[4:]
    r, s = lax.axis_index("row"), lax.axis_index("sub")
    q = lax.axis_index("aux") * 2 + s
    size, orbitals = density.shape
    cut = orbitals // 128
    h, odd = r // 2, r % 2 == 1
    rows_of = lambda k: pl.ds(pl.multiple_of((r ^ k) * size, size), size)
    at = share * cut * size

    def keep(k, left, right):
        for x, value in enumerate((left, right)):
            high, lower = split(value)
            dh[rows_of(k), x * 128:(x + 1) * 128] = high
            dl[rows_of(k), x * 128:(x + 1) * 128] = lower

    mine = [density[:, x * 128:(x + 1) * 128] for x in range(2)]
    beside = [one[at + x * size:at + (x + 1) * size, :] for x in range(2)]
    keep(0, *mine)
    keep(1, *beside)
    a, b = [jnp.where(h == 0, x[1], x[0]) for x in (mine, beside)]
    across = jnp.transpose(jnp.concatenate([jnp.where(odd, b, a), jnp.where(odd, a, b)], axis=0))
    middle = share * size
    came = [ref[middle:middle + size // 2, :] for ref in (two, two_other)]
    here = jnp.where(s == 0, jnp.concatenate(came, axis=0), jnp.concatenate(came[::-1], axis=0))
    mirror = jnp.transpose(jnp.concatenate([here, here], axis=0))
    mirror = jnp.where(odd, mirror[:size], mirror[size:])
    corner = unfold(three[at:, :])
    corner = jnp.where(odd, corner, pltpu.roll(corner, 64, 1))
    low = lax.broadcasted_iota(jnp.int32, (size, 128), 1) < 64
    last = jnp.where(low ^ odd, mirror, corner)
    for k, inner, outer in (
        (2, here, jnp.where(odd, across[size:], across[:size])),
        (3, last, jnp.where(odd, across[:size], across[size:])),
    ):
        keep(k, jnp.where(h == 0, outer, inner), jnp.where(h == 0, inner, outer))
    for k, chunk in ((0, own), (1, one), (3, three)):
        for j in range(share):
            for x in range(cut):
                at = (j * cut + x) * size
                high, lower = split(chunk[at:at + size, :])
                bh[j, rows_of(k), x * 128:(x + 1) * 128] = high
                bl[j, rows_of(k), x * 128:(x + 1) * 128] = lower
    at = middle + size // 2
    spots = [
        [jnp.broadcast_to(ref[at + i:at + i + 1, :], (size, 128)) for i in range(2)] for ref in (two_other, two)
    ]
    for j in range(share):
        values = [jnp.zeros((size, 128), F32)] * cut
        for d, ref in enumerate((two, two_other)):
            x = j * size + (0 if d else at + 8)
            values = spread(spots[d], ref[x:x + size, :], values)
        for x, value in enumerate(values):
            high, lower = split(value)
            bh[j, rows_of(2), x * 128:(x + 1) * 128] = high
            bl[j, rows_of(2), x * 128:(x + 1) * 128] = lower
    side = lambda *parts: jnp.concatenate(parts, axis=1)
    whole = jnp.concatenate([dh[...], dl[...], dh[...]], axis=0)
    lefts, rights = [], []
    for j in range(share):
        b1, b2 = bh[j], bl[j]
        c1, c2 = split(jnp.dot(side(b1, b1, b2), whole, preferred_element_type=F32))
        lefts += [c1, c1, c2]
        rights += [b1, b2, b1]
    result = lax.dot_general(
        side(*lefts), side(*rights), (((1,), (1,)), ((), ())), preferred_element_type=F32
    )
    total[...] = result
    for dq in range(4):
        outs[dq][...] = total[pl.ds(pl.multiple_of((q ^ dq) * size, size), size), :]


def cut_kernel(*refs):
    ins, outs = refs[:4], refs[4:]
    r = lax.axis_index("row")
    value = ins[0][...] + ins[1][...] + (ins[2][...] + ins[3][...])
    for k in range(4):
        outs[k][:value.shape[0] // 2, :] = fold(column_block(value, r ^ k))


def final_kernel(kept, one, two, three, out):
    half = out.shape[0] // 2
    value = kept[...] + one[:half, :] + (two[:half, :] + three[:half, :])
    out[...] = jnp.transpose(unfold(value))[:out.shape[0], :]


def dealt_body(factor, density, screen):
    block_size, orbitals = density.shape
    aux_local = factor.shape[1]
    share = aux_local // 8
    packed = share * orbitals // 128 * block_size
    flat = factor.reshape(block_size * aux_local, factor.shape[2])
    row = lambda x, k: swap(x, "row", 4, k)
    core = lambda x: swap(x, "sub", 2, 1)
    other = core(flat)
    raw, mine = call(
        functools.partial(near_kernel, share, block_size),
        [(2 * share * block_size, 128), flat.shape],
        ins=[HBM],
        scratch=[pltpu.SemaphoreType.DMA((2,))],
        limit=FIRST,
    )(flat)
    extended = (raw.shape[0] + block_size // 2 + 8, 128)
    passed = (extended[0] - share * block_size, 128)
    other_screen = core(screen)
    two = row(call(extend_kernel, [extended], count=3)(raw, other_screen, density)[0], 2)
    own, one, three = call(
        functools.partial(far_kernel, share),
        [(packed + more, 128) for more in (0, orbitals // 2, block_size // 2)],
        count=5,
    )(screen, other_screen, mine, other, density)
    three, one = row(three, 3), row(one, 1)
    parts = call(
        functools.partial(fock_kernel, share),
        [(block_size, orbitals)] * 4,
        scratch=[
            pltpu.VMEM((orbitals, orbitals), BF16),
            pltpu.VMEM((orbitals, orbitals), BF16),
            pltpu.VMEM((share, orbitals, orbitals), BF16),
            pltpu.VMEM((share, orbitals, orbitals), BF16),
            pltpu.VMEM((orbitals, orbitals), F32),
        ],
        count=6,
    )(own, one, two, core(call(pass_kernel, [passed], count=1)(two)[0]), three, density)
    sums = [parts[0]] + [swap(parts[k], ("aux", "sub"), 4, k) for k in (1, 2, 3)]
    cuts = call(cut_kernel, [(block_size // 2 + more, 2 * block_size) for more in (0, 0, 8, 16)], count=4)(*sums)
    moved = [row(cuts[k], k) for k in (1, 2, 3)]
    return call(final_kernel, [(block_size, block_size)], count=4)(cuts[0], *moved)[0]


def pair_block(tiled, block_rows, block_cols):
    block_size = tiled.shape[0]
    picked = jnp.take(tiled, block_cols, axis=2)
    others = block_rows.reshape(
        block_rows.shape[0], block_rows.shape[1], block_cols.shape[0], block_size
    )
    return jnp.einsum(
        "ipsl,jpsl->ij", picked, others, precision=precise, preferred_element_type=jnp.float32
    )


def gathered_body(factor, density, screen):
    block_size = density.shape[0]
    orbitals = density.shape[1]
    nblocks = orbitals // block_size
    aux_local = factor.shape[1]
    own_block = lax.axis_index("row")
    full_rows, full_screen = (
        lax.all_gather(factor, "sub", axis=2, tiled=True),
        lax.all_gather(screen, "sub", axis=1, tiled=True),
    )
    whole = lax.all_gather(density, "row", axis=0, tiled=True)
    stacked = whole.reshape(nblocks, block_size, orbitals)
    panel = jnp.take(stacked, screen[0], axis=0).reshape(-1, orbitals)
    contracted = jnp.einsum(
        "ipk,kl->ipl", factor, panel, precision=precise, preferred_element_type=jnp.float32
    )
    tiled = contracted.reshape(block_size, aux_local, nblocks, block_size)
    zero_block = jnp.zeros((block_size, block_size), jnp.float32)
    rows_piece = lax.all_gather(full_rows[None], "row", axis=0, tiled=True)
    screen_piece = lax.all_gather(full_screen, "row", axis=0, tiled=True)
    count = rows_piece.shape[0]

    def single(member):
        offset, rows_one, screen_one = member
        return lax.cond(
            offset >= own_block, lambda: pair_block(tiled, rows_one, screen_one), lambda: zero_block
        )

    computed = lax.map(single, (jnp.arange(count, dtype=jnp.int32), rows_piece, screen_piece))
    updated = jnp.transpose(computed, (1, 0, 2))
    keep_mask = (jnp.arange(nblocks, dtype=jnp.int32) != own_block).astype(jnp.float32)
    received = lax.all_to_all(updated, "row", split_axis=1, concat_axis=1, tiled=True)
    mirrored = jnp.transpose(received, (2, 1, 0)) * keep_mask[None, :, None]
    partial_value = (updated + mirrored).reshape(block_size, orbitals)
    return lax.psum_scatter(partial_value, ("aux", "sub"), scatter_dimension=1, tiled=True)


def solution(mesh):
    sizes = tuple(mesh.shape[a] for a in ("row", "aux", "sub"))

    def body(factor, density, screen):
        nrow, naux, nsub = sizes
        block_size, orbitals = density.shape
        fits = (
            naux * nsub == 4
            and nsub == 2
            and nrow == 4
            and block_size == 64
            and orbitals == nrow * block_size
            and factor.shape[2] == 128
            and factor.shape[1] % (nrow * nsub * 2) == 0
        )
        if fits:
            return dealt_body(factor, density, screen)
        return gathered_body(factor, density, screen)

    return jax.shard_map(
        body,
        mesh=mesh,
        in_specs=(
            P(("dom", "row"), "aux", "sub"),
            P(("dom", "row"), None),
            P(("dom", "row"), "sub"),
        ),
        out_specs=P(("dom", "row"), ("aux", "sub")),
        check_vma=False,
    )
```

```python
import functools

import jax
import jax.numpy as jnp
from jax import lax
from jax.experimental import pallas as pl
from jax.experimental.pallas import tpu as pltpu
from jax.sharding import PartitionSpec as P

precise = lax.Precision.HIGHEST
VMEM = pl.BlockSpec(memory_space=pltpu.VMEM)
HBM = pl.BlockSpec(memory_space=pltpu.HBM)
FIRST = 54272 * 1024
F32 = jnp.float32
BF16 = jnp.bfloat16


def call(kernel, outs, scratch=(), ins=None, count=0, limit=12 << 20, halved=()):
    return pl.pallas_call(
        kernel,
        out_shape=tuple(jax.ShapeDtypeStruct(s, t) for x, t in ((outs, F32), (halved, BF16)) for s in x),
        in_specs=ins if ins is not None else [VMEM] * count,
        out_specs=(VMEM,) * (len(outs) + len(halved)),
        scratch_shapes=list(scratch),
        compiler_params=pltpu.CompilerParams(vmem_limit_bytes=limit),
    )


def swap(x, axes, size, k):
    return lax.ppermute(x, axes, [(a, a ^ k) for a in range(size)])


def split(x):
    high = x.astype(BF16)
    return high, (x - high.astype(F32)).astype(BF16)


def lanes(ref, size):
    low = lax.broadcasted_iota(jnp.int32, (size, 128), 1) < 64
    a, b = [jnp.broadcast_to(ref[0:1, i:i + 1], (size, 128)) for i in range(2)]
    return [jnp.where(low, a, b), jnp.where(low, b, a)]


def spread(places, part, start):
    size = part.shape[0]
    turned = pltpu.roll(part, 64, 1)
    half = jnp.where(lax.broadcasted_iota(jnp.int32, (size, 128), 1) < 64, 0, 1)
    columns = []
    for h, value in enumerate(start):
        block = (half + 2 * h).astype(places[0].dtype)
        value = jnp.where(places[0] == block, part, value)
        columns.append(jnp.where(places[1] == block, turned, value))
    return columns


def fold(block):
    size = block.shape[0]
    low = lax.broadcasted_iota(jnp.int32, (size // 2, 128), 1) < 64
    return jnp.where(low, block[:size // 2], pltpu.roll(block, 64, 1)[size // 2:])


def unfold(folded):
    return jnp.concatenate([folded, pltpu.roll(folded, 64, 1)], axis=0)


def half_of(value, h):
    return jnp.where(h == 0, value[:, :128], value[:, 128:])


def column_block(value, b):
    picked = half_of(value, b // 2)
    return jnp.where(b % 2 == 1, pltpu.roll(picked, 64, 1), picked)


def near_kernel(share, size, own_hbm, raw, own, sems):
    r, s = lax.axis_index("row"), lax.axis_index("sub")
    aux_local = own.shape[0] // size
    part_size = size // 2
    length = part_size * aux_local
    halves = [pl.ds(i * length, length) for i in range(2)]
    copies = [pltpu.make_async_copy(own_hbm.at[x], own.at[x], sems.at[i]) for i, x in enumerate(halves)]
    for copy in copies:
        copy.start()
    for i in range(2):
        copies[i].wait()
        for d in range(2):
            for j in range(share):
                p = ((r ^ 2) * 2 + (s ^ d)) * share + j + i * length
                at = ((1 - d) * share + j) * size + i * part_size
                raw[at:at + part_size, :] = own[pl.ds(p, part_size, stride=aux_local), :]


def extend_kernel(raw, other_ref, density_ref, out):
    r, s = lax.axis_index("row"), lax.axis_index("sub")
    at, rows = raw.shape[0] // 2, density_ref.shape[0] // 2
    out[:at, :] = raw[:at, :]
    some = pl.ds(pl.multiple_of(s * rows, rows), rows)
    out[at:at + rows, :] = half_of(density_ref[some, :], r // 2)
    direct, turned = lanes(other_ref, 8)
    even = lax.broadcasted_iota(jnp.int32, (8, 128), 0) % 2 == 0
    out[at + rows:at + rows + 8, :] = jnp.where(even, direct, turned).astype(F32)
    out[at + rows + 8:, :] = raw[at:, :]


def pass_kernel(two, out):
    out[...] = two[:out.shape[0], :]


def far_kernel(share, screen_ref, other_ref, own_ref, par_ref, density_ref, *outs):
    r, s = lax.axis_index("row"), lax.axis_index("sub")
    size, orbitals = density_ref.shape
    aux_local = par_ref.shape[0] // size
    sources = [(lanes(places, size), part) for places, part in ((screen_ref, own_ref), (other_ref, par_ref))]
    cut = orbitals // 128
    for k, out in zip((0, 1, 3), outs):
        for j in range(share):
            p = ((r ^ k) * 2 + s) * share + j
            values = [jnp.zeros((size, 128), F32)] * cut
            for places, part in sources:
                values = spread(places, part[pl.ds(p, size, stride=aux_local), :], values)
            for h, value in enumerate(values):
                at = (j * cut + h) * size
                out[at:at + size, :] = value
    at = share * cut * size
    density = density_ref[...]
    for h in range(cut):
        outs[1][at + h * size:at + (h + 1) * size, :] = density[:, h * 128:(h + 1) * 128]
    outs[2][at:, :] = fold(column_block(density, r))


def keep_parts(refs, j, at, values):
    for x, value in enumerate(values):
        for ref, part in zip(refs, split(value)):
            ref[j, at:at + value.shape[0], x * 128:(x + 1) * 128] = part


def chunk_parts(chunk, j, size, cut):
    return [chunk[(j * cut + x) * size:(j * cut + x + 1) * size, :] for x in range(cut)]


def early_kernel(own, one, two, two_other, density, eh, el, dh, dl):
    r, s = lax.axis_index("row"), lax.axis_index("sub")
    size, orbitals = density.shape
    share, cut = eh.shape[0], orbitals // 128
    h, odd = r // 2, r % 2 == 1

    def keep(k, left, right):
        rows = pl.ds(pl.multiple_of((r ^ k) * size, size), size)
        for x, value in enumerate((left, right)):
            high, lower = split(value)
            dh[rows, x * 128:(x + 1) * 128] = high
            dl[rows, x * 128:(x + 1) * 128] = lower

    at = share * cut * size
    mine = [density[:, x * 128:(x + 1) * 128] for x in range(2)]
    beside = [one[at + x * size:at + (x + 1) * size, :] for x in range(2)]
    keep(0, *mine)
    keep(1, *beside)
    a, b = [jnp.where(h == 0, x[1], x[0]) for x in (mine, beside)]
    across = jnp.transpose(jnp.concatenate([jnp.where(odd, b, a), jnp.where(odd, a, b)], axis=0))
    middle = share * size
    came = [ref[middle:middle + size // 2, :] for ref in (two, two_other)]
    here = jnp.where(s == 0, jnp.concatenate(came, axis=0), jnp.concatenate(came[::-1], axis=0))
    mirror = jnp.transpose(jnp.concatenate([here, here], axis=0))
    mirror = jnp.where(odd, mirror[:size], mirror[size:])
    for k, inner, outer in (
        (2, here, jnp.where(odd, across[size:], across[:size])),
        (3, mirror, jnp.where(odd, across[:size], across[size:])),
    ):
        keep(k, jnp.where(h == 0, outer, inner), jnp.where(h == 0, inner, outer))
    at = middle + size // 2
    spots = [
        [jnp.broadcast_to(ref[at + i:at + i + 1, :], (size, 128)) for i in range(2)] for ref in (two_other, two)
    ]
    for j in range(share):
        values = [jnp.zeros((size, 128), F32)] * cut
        for d, ref in enumerate((two, two_other)):
            x = j * size + (0 if d else at + 8)
            values = spread(spots[d], ref[x:x + size, :], values)
        for i, parts in enumerate((chunk_parts(own, j, size, cut), values, chunk_parts(one, j, size, cut))):
            keep_parts((eh, el), j, i * size, parts)


def fock_kernel(eh, el, fh, fl, three, *refs):
    outs, (dh, dl, lh, ll, total) = refs[:4], refs[4:]
    r = lax.axis_index("row")
    q = lax.axis_index("aux") * 2 + lax.axis_index("sub")
    share, orbitals = eh.shape[0], fh.shape[0]
    size, cut = orbitals - eh.shape[1], orbitals // 128
    h, odd = r // 2, r % 2 == 1
    corner = unfold(three[share * cut * size:, :])
    low = lax.broadcasted_iota(jnp.int32, (size, 128), 1) < 64
    corner = split(jnp.where(low, corner, pltpu.roll(corner, 64, 1)))
    rows = pl.ds(pl.multiple_of((r ^ 3) * size, size), size)
    for old, new, part in zip((fh, fl), (dh, dl), corner):
        new[...] = old[...]
        for x in range(cut):
            columns = slice(x * 128, (x + 1) * 128)
            other = jnp.logical_or(low ^ odd, h == x)
            new[rows, columns] = jnp.where(other, old[rows, columns].astype(F32), part.astype(F32)).astype(BF16)
    side = lambda *parts: jnp.concatenate(parts, axis=1)
    whole = jnp.concatenate([dh[...], dl[...], dh[...]], axis=0)
    lefts, rights = [], []
    for j in range(share):
        keep_parts((lh, ll), j, 0, chunk_parts(three, j, size, cut))
        b1, b2 = [jnp.concatenate([x[j], y[j]], axis=0) for x, y in ((eh, lh), (el, ll))]
        c1, c2 = split(jnp.dot(side(b1, b1, b2), whole, preferred_element_type=F32))
        lefts += [c1, c1, c2]
        rights += [b1, b2, b1]
    total[...] = lax.dot_general(
        side(*lefts), side(*rights), (((1,), (1,)), ((), ())), preferred_element_type=F32
    )
    for dq in range(4):
        k = q ^ dq ^ r
        start = pl.multiple_of((k % 2 * 2 + k // 2) * size, size)
        outs[dq][...] = total[pl.ds(start, size), :]


def cut_kernel(*refs):
    ins, outs = refs[:4], refs[4:]
    value = ins[0][...] + ins[1][...] + (ins[2][...] + ins[3][...])
    for k in range(4):
        outs[k][:value.shape[0] // 2, :] = fold(column_block(value, k % 2 * 2 + k // 2))


def final_kernel(kept, one, two, three, out):
    half = out.shape[0] // 2
    value = kept[...] + one[:half, :] + (two[:half, :] + three[:half, :])
    out[...] = jnp.transpose(unfold(value))[:out.shape[0], :]


def dealt_body(factor, density, screen):
    block_size, orbitals = density.shape
    aux_local = factor.shape[1]
    share = aux_local // 8
    packed = share * orbitals // 128 * block_size
    flat = factor.reshape(block_size * aux_local, factor.shape[2])
    row = lambda x, k: swap(x, "row", 4, k)
    core = lambda x: swap(x, "sub", 2, 1)
    other = core(flat)
    raw, mine = call(
        functools.partial(near_kernel, share, block_size),
        [(2 * share * block_size, 128), flat.shape],
        ins=[HBM],
        scratch=[pltpu.SemaphoreType.DMA((2,))],
        limit=FIRST,
    )(flat)
    extended = (raw.shape[0] + block_size // 2 + 8, 128)
    passed = (extended[0] - share * block_size, 128)
    other_screen = core(screen)
    two = row(call(extend_kernel, [extended], count=3)(raw, other_screen, density)[0], 2)
    own, one, three = call(
        functools.partial(far_kernel, share),
        [(packed + more, 128) for more in (0, orbitals // 2, block_size // 2)],
        count=5,
    )(screen, other_screen, mine, other, density)
    three, one = row(three, 3), row(one, 1)
    two_other = core(call(pass_kernel, [passed], count=1)(two)[0])
    whole = (orbitals, orbitals)
    early = call(
        early_kernel, [], count=5, halved=((share, orbitals - block_size, orbitals),) * 2 + (whole,) * 2
    )(own, one, two, two_other, density)
    parts = call(
        fock_kernel,
        [(block_size, orbitals)] * 4,
        scratch=[
            pltpu.VMEM(whole, BF16),
            pltpu.VMEM(whole, BF16),
            pltpu.VMEM((share, block_size, orbitals), BF16),
            pltpu.VMEM((share, block_size, orbitals), BF16),
            pltpu.VMEM(whole, F32),
        ],
        count=5,
    )(*early, three)
    sums = [parts[0]] + [swap(parts[k], ("aux", "sub"), 4, k) for k in (1, 2, 3)]
    cuts = call(cut_kernel, [(block_size // 2 + more, 2 * block_size) for more in (0, 0, 8, 16)], count=4)(*sums)
    moved = [row(cuts[k], k) for k in (1, 2, 3)]
    return call(final_kernel, [(block_size, block_size)], count=4)(cuts[0], *moved)[0]


def pair_block(tiled, block_rows, block_cols):
    block_size = tiled.shape[0]
    picked = jnp.take(tiled, block_cols, axis=2)
    others = block_rows.reshape(
        block_rows.shape[0], block_rows.shape[1], block_cols.shape[0], block_size
    )
    return jnp.einsum(
        "ipsl,jpsl->ij", picked, others, precision=precise, preferred_element_type=jnp.float32
    )


def gathered_body(factor, density, screen):
    block_size = density.shape[0]
    orbitals = density.shape[1]
    nblocks = orbitals // block_size
    aux_local = factor.shape[1]
    own_block = lax.axis_index("row")
    full_rows, full_screen = (
        lax.all_gather(factor, "sub", axis=2, tiled=True),
        lax.all_gather(screen, "sub", axis=1, tiled=True),
    )
    whole = lax.all_gather(density, "row", axis=0, tiled=True)
    stacked = whole.reshape(nblocks, block_size, orbitals)
    panel = jnp.take(stacked, screen[0], axis=0).reshape(-1, orbitals)
    contracted = jnp.einsum(
        "ipk,kl->ipl", factor, panel, precision=precise, preferred_element_type=jnp.float32
    )
    tiled = contracted.reshape(block_size, aux_local, nblocks, block_size)
    zero_block = jnp.zeros((block_size, block_size), jnp.float32)
    rows_piece = lax.all_gather(full_rows[None], "row", axis=0, tiled=True)
    screen_piece = lax.all_gather(full_screen, "row", axis=0, tiled=True)
    count = rows_piece.shape[0]

    def single(member):
        offset, rows_one, screen_one = member
        return lax.cond(
            offset >= own_block, lambda: pair_block(tiled, rows_one, screen_one), lambda: zero_block
        )

    computed = lax.map(single, (jnp.arange(count, dtype=jnp.int32), rows_piece, screen_piece))
    updated = jnp.transpose(computed, (1, 0, 2))
    keep_mask = (jnp.arange(nblocks, dtype=jnp.int32) != own_block).astype(jnp.float32)
    received = lax.all_to_all(updated, "row", split_axis=1, concat_axis=1, tiled=True)
    mirrored = jnp.transpose(received, (2, 1, 0)) * keep_mask[None, :, None]
    partial_value = (updated + mirrored).reshape(block_size, orbitals)
    return lax.psum_scatter(partial_value, ("aux", "sub"), scatter_dimension=1, tiled=True)


def solution(mesh):
    sizes = tuple(mesh.shape[a] for a in ("row", "aux", "sub"))

    def body(factor, density, screen):
        nrow, naux, nsub = sizes
        block_size, orbitals = density.shape
        fits = (
            naux * nsub == 4
            and nsub == 2
            and nrow == 4
            and block_size == 64
            and orbitals == nrow * block_size
            and factor.shape[2] == 128
            and factor.shape[1] % (nrow * nsub * 2) == 0
        )
        if fits:
            return dealt_body(factor, density, screen)
        return gathered_body(factor, density, screen)

    return jax.shard_map(
        body,
        mesh=mesh,
        in_specs=(
            P(("dom", "row"), "aux", "sub"),
            P(("dom", "row"), None),
            P(("dom", "row"), "sub"),
        ),
        out_specs=P(("dom", "row"), ("aux", "sub")),
        check_vma=False,
    )
```

```python
import functools

import jax
import jax.numpy as jnp
from jax import lax
from jax.experimental import pallas as pl
from jax.experimental.pallas import tpu as pltpu
from jax.sharding import PartitionSpec as P

precise = lax.Precision.HIGHEST
VMEM = pl.BlockSpec(memory_space=pltpu.VMEM)
HBM = pl.BlockSpec(memory_space=pltpu.HBM)
FIRST = 54272 * 1024
F32 = jnp.float32
BF16 = jnp.bfloat16


def call(kernel, outs, scratch=(), ins=None, count=0, limit=12 << 20, halved=()):
    return pl.pallas_call(
        kernel,
        out_shape=tuple(jax.ShapeDtypeStruct(s, t) for x, t in ((outs, F32), (halved, BF16)) for s in x),
        in_specs=ins if ins is not None else [VMEM] * count,
        out_specs=(VMEM,) * (len(outs) + len(halved)),
        scratch_shapes=list(scratch),
        compiler_params=pltpu.CompilerParams(vmem_limit_bytes=limit),
    )


def swap(x, axes, size, k):
    return lax.ppermute(x, axes, [(a, a ^ k) for a in range(size)])


def split(x):
    high = x.astype(BF16)
    return high, (x - high.astype(F32)).astype(BF16)


def lanes(ref, size):
    low = lax.broadcasted_iota(jnp.int32, (size, 128), 1) < 64
    a, b = [jnp.broadcast_to(ref[0:1, i:i + 1], (size, 128)) for i in range(2)]
    return [jnp.where(low, a, b), jnp.where(low, b, a)]


def spread(places, part, start):
    size = part.shape[0]
    turned = pltpu.roll(part, 64, 1)
    half = jnp.where(lax.broadcasted_iota(jnp.int32, (size, 128), 1) < 64, 0, 1)
    columns = []
    for h, value in enumerate(start):
        block = (half + 2 * h).astype(places[0].dtype)
        value = jnp.where(places[0] == block, part, value)
        columns.append(jnp.where(places[1] == block, turned, value))
    return columns


def fold(block):
    size = block.shape[0]
    low = lax.broadcasted_iota(jnp.int32, (size // 2, 128), 1) < 64
    return jnp.where(low, block[:size // 2], pltpu.roll(block, 64, 1)[size // 2:])


def unfold(folded):
    return jnp.concatenate([folded, pltpu.roll(folded, 64, 1)], axis=0)


def half_of(value, h):
    return jnp.where(h == 0, value[:, :128], value[:, 128:])


def column_block(value, b):
    picked = half_of(value, b // 2)
    return jnp.where(b % 2 == 1, pltpu.roll(picked, 64, 1), picked)


def near_kernel(share, size, own_hbm, raw, own, sems):
    r, s = lax.axis_index("row"), lax.axis_index("sub")
    aux_local = own.shape[0] // size
    part_size = size // 2
    length = part_size * aux_local
    halves = [pl.ds(i * length, length) for i in range(2)]
    copies = [pltpu.make_async_copy(own_hbm.at[x], own.at[x], sems.at[i]) for i, x in enumerate(halves)]
    for copy in copies:
        copy.start()
    for i in range(2):
        copies[i].wait()
        for d in range(2):
            for j in range(share):
                p = ((r ^ 2) * 2 + (s ^ d)) * share + j + i * length
                at = ((1 - d) * share + j) * size + i * part_size
                raw[at:at + part_size, :] = own[pl.ds(p, part_size, stride=aux_local), :]


def extend_kernel(raw, other_ref, density_ref, out):
    r, s = lax.axis_index("row"), lax.axis_index("sub")
    at, rows = raw.shape[0] // 2, density_ref.shape[0] // 2
    out[:at, :] = raw[:at, :]
    some = pl.ds(pl.multiple_of(s * rows, rows), rows)
    out[at:at + rows, :] = half_of(density_ref[some, :], r // 2)
    direct, turned = lanes(other_ref, 8)
    even = lax.broadcasted_iota(jnp.int32, (8, 128), 0) % 2 == 0
    out[at + rows:at + rows + 8, :] = jnp.where(even, direct, turned).astype(F32)
    out[at + rows + 8:, :] = raw[at:, :]


def pass_kernel(two, out):
    out[...] = two[:out.shape[0], :]


def far_kernel(share, screen_ref, other_ref, own_ref, par_ref, density_ref, *outs):
    r, s = lax.axis_index("row"), lax.axis_index("sub")
    size, orbitals = density_ref.shape
    aux_local = par_ref.shape[0] // size
    sources = [(lanes(places, size), part) for places, part in ((screen_ref, own_ref), (other_ref, par_ref))]
    cut = orbitals // 128
    for k, out in zip((0, 1, 3), outs):
        for j in range(share):
            p = ((r ^ k) * 2 + s) * share + j
            values = [jnp.zeros((size, 128), F32)] * cut
            for places, part in sources:
                values = spread(places, part[pl.ds(p, size, stride=aux_local), :], values)
            for h, value in enumerate(values):
                at = (j * cut + h) * size
                out[at:at + size, :] = value
    at = share * cut * size
    density = density_ref[...]
    for h in range(cut):
        outs[1][at + h * size:at + (h + 1) * size, :] = density[:, h * 128:(h + 1) * 128]
    outs[2][at:, :] = fold(column_block(density, r))


def keep_parts(refs, j, at, values):
    for x, value in enumerate(values):
        for ref, part in zip(refs, split(value)):
            ref[j, at:at + value.shape[0], x * 128:(x + 1) * 128] = part


def chunk_parts(chunk, j, size, cut):
    return [chunk[(j * cut + x) * size:(j * cut + x + 1) * size, :] for x in range(cut)]


def early_kernel(own, one, two, two_other, density, eh, el, dh, dl):
    r, s = lax.axis_index("row"), lax.axis_index("sub")
    size, orbitals = density.shape
    share, cut = eh.shape[0], orbitals // 128
    h, odd = r // 2, r % 2 == 1

    def keep(k, left, right):
        rows = pl.ds(pl.multiple_of((r ^ k) * size, size), size)
        for x, value in enumerate((left, right)):
            high, lower = split(value)
            dh[rows, x * 128:(x + 1) * 128] = high
            dl[rows, x * 128:(x + 1) * 128] = lower

    at = share * cut * size
    mine = [density[:, x * 128:(x + 1) * 128] for x in range(2)]
    beside = [one[at + x * size:at + (x + 1) * size, :] for x in range(2)]
    keep(0, *mine)
    keep(1, *beside)
    a, b = [jnp.where(h == 0, x[1], x[0]) for x in (mine, beside)]
    across = jnp.transpose(jnp.concatenate([jnp.where(odd, b, a), jnp.where(odd, a, b)], axis=0))
    middle = share * size
    came = [ref[middle:middle + size // 2, :] for ref in (two, two_other)]
    here = jnp.where(s == 0, jnp.concatenate(came, axis=0), jnp.concatenate(came[::-1], axis=0))
    mirror = jnp.transpose(jnp.concatenate([here, here], axis=0))
    mirror = jnp.where(odd, mirror[:size], mirror[size:])
    for k, inner, outer in (
        (2, here, jnp.where(odd, across[size:], across[:size])),
        (3, mirror, jnp.where(odd, across[:size], across[size:])),
    ):
        keep(k, jnp.where(h == 0, outer, inner), jnp.where(h == 0, inner, outer))
    at = middle + size // 2
    spots = [
        [jnp.broadcast_to(ref[at + i:at + i + 1, :], (size, 128)) for i in range(2)] for ref in (two_other, two)
    ]
    for j in range(share):
        values = [jnp.zeros((size, 128), F32)] * cut
        for d, ref in enumerate((two, two_other)):
            x = j * size + (0 if d else at + 8)
            values = spread(spots[d], ref[x:x + size, :], values)
        for i, parts in enumerate((chunk_parts(own, j, size, cut), values, chunk_parts(one, j, size, cut))):
            keep_parts((eh, el), j, i * size, parts)


def fock_rows(a, bh, bl, dh, dl, total, outs):
    s = lax.axis_index("sub")
    count, size = total.shape[0], outs[0].shape[0]
    rows = pl.ds(pl.multiple_of(a * count, count), count)
    side = lambda *parts: jnp.concatenate(parts, axis=1)
    whole = jnp.concatenate([dh[...], dl[...], dh[...]], axis=0)
    lefts, rights = [], []
    for j in range(bh.shape[0]):
        high, lower = bh[j, rows, :], bl[j, rows, :]
        c1, c2 = split(jnp.dot(side(high, high, lower), whole, preferred_element_type=F32))
        lefts += [c1, c1, c2]
        rights += [bh[j], bl[j], bh[j]]
    total[...] = lax.dot_general(
        side(*lefts), side(*rights), (((1,), (1,)), ((), ())), preferred_element_type=F32
    )
    for d, out in enumerate(outs):
        out[...] = total[pl.ds(pl.multiple_of((s ^ d) * size, size), size), :]


def leave_kernel(eh, el, fh, fl, three, same, cross, bh, bl, dh, dl, total):
    r = lax.axis_index("row")
    share, orbitals = eh.shape[0], fh.shape[0]
    size, cut = orbitals - eh.shape[1], orbitals // 128
    h, odd = r // 2, r % 2 == 1
    corner = unfold(three[share * cut * size:, :])
    low = lax.broadcasted_iota(jnp.int32, (size, 128), 1) < 64
    corner = split(jnp.where(low, corner, pltpu.roll(corner, 64, 1)))
    rows_of = lambda k: pl.ds(pl.multiple_of((r ^ k) * size, size), size)
    rows = rows_of(3)
    for old, new, part in zip((fh, fl), (dh, dl), corner):
        new[...] = old[...]
        for x in range(cut):
            columns = slice(x * 128, (x + 1) * 128)
            other = jnp.logical_or(low ^ odd, h == x)
            new[rows, columns] = jnp.where(other, old[rows, columns].astype(F32), part.astype(F32)).astype(BF16)
    for j in range(share):
        for i, k in enumerate((0, 2, 1)):
            for old, new in ((eh, bh), (el, bl)):
                new[j, rows_of(k), :] = old[j, i * size:(i + 1) * size, :]
        for x, value in enumerate(chunk_parts(three, j, size, cut)):
            for new, part in zip((bh, bl), split(value)):
                new[j, rows, x * 128:(x + 1) * 128] = part
    fock_rows(1 - lax.axis_index("aux"), bh, bl, dh, dl, total, (same, cross))


def stay_kernel(bh, bl, dh, dl, same, upper, lower, total, whole):
    fock_rows(lax.axis_index("aux"), bh, bl, dh, dl, total, (same, whole))
    half = upper.shape[0]
    upper[...] = whole[:half, :]
    lower[...] = whole[half:, :]


def cut_kernel(*refs):
    ins, outs = refs[:5], refs[5:]
    r = lax.axis_index("row")
    near = jnp.concatenate([ins[3][...], ins[4][...]], axis=0)
    value = ins[0][...] + near + (ins[1][...] + ins[2][...])
    for k in range(4):
        outs[k][:value.shape[0] // 2, :] = fold(column_block(value, r ^ k))


def final_kernel(kept, one, two, three, out):
    half = out.shape[0] // 2
    value = kept[...] + one[:half, :] + (two[:half, :] + three[:half, :])
    out[...] = jnp.transpose(unfold(value))[:out.shape[0], :]


def dealt_body(factor, density, screen):
    block_size, orbitals = density.shape
    aux_local = factor.shape[1]
    share = aux_local // 8
    packed = share * orbitals // 128 * block_size
    flat = factor.reshape(block_size * aux_local, factor.shape[2])
    row = lambda x, k: swap(x, "row", 4, k)
    core = lambda x: swap(x, "sub", 2, 1)
    other = core(flat)
    raw, mine = call(
        functools.partial(near_kernel, share, block_size),
        [(2 * share * block_size, 128), flat.shape],
        ins=[HBM],
        scratch=[pltpu.SemaphoreType.DMA((2,))],
        limit=FIRST,
    )(flat)
    extended = (raw.shape[0] + block_size // 2 + 8, 128)
    passed = (extended[0] - share * block_size, 128)
    other_screen = core(screen)
    two = row(call(extend_kernel, [extended], count=3)(raw, other_screen, density)[0], 2)
    own, one, three = call(
        functools.partial(far_kernel, share),
        [(packed + more, 128) for more in (0, orbitals // 2, block_size // 2)],
        count=5,
    )(screen, other_screen, mine, other, density)
    three, one = row(three, 3), row(one, 1)
    two_other = core(call(pass_kernel, [passed], count=1)(two)[0])
    whole = (orbitals, orbitals)
    early = call(
        early_kernel, [], count=5, halved=((share, orbitals - block_size, orbitals),) * 2 + (whole,) * 2
    )(own, one, two, two_other, density)
    block = (block_size, orbitals)
    scratch = [pltpu.VMEM((2 * block_size, orbitals), F32)]
    far_same, far_cross, *pieces = call(
        leave_kernel, [block] * 2, scratch, count=5, halved=((share,) + whole,) * 2 + (whole,) * 2
    )(*early, three)
    piece = (block_size // 2, orbitals)
    same, upper, lower = call(stay_kernel, [block, piece, piece], scratch + [pltpu.VMEM(block, F32)], count=4)(*pieces)
    sums = [same, swap(far_same, "aux", 2, 1), swap(far_cross, ("aux", "sub"), 4, 3), core(upper), core(lower)]
    cuts = call(cut_kernel, [(block_size // 2 + more, 2 * block_size) for more in (0, 0, 8, 16)], count=5)(*sums)
    moved = [row(cuts[k], k) for k in (1, 2, 3)]
    return call(final_kernel, [(block_size, block_size)], count=4)(cuts[0], *moved)[0]


def pair_block(tiled, block_rows, block_cols):
    block_size = tiled.shape[0]
    picked = jnp.take(tiled, block_cols, axis=2)
    others = block_rows.reshape(
        block_rows.shape[0], block_rows.shape[1], block_cols.shape[0], block_size
    )
    return jnp.einsum(
        "ipsl,jpsl->ij", picked, others, precision=precise, preferred_element_type=jnp.float32
    )


def gathered_body(factor, density, screen):
    block_size = density.shape[0]
    orbitals = density.shape[1]
    nblocks = orbitals // block_size
    aux_local = factor.shape[1]
    own_block = lax.axis_index("row")
    full_rows, full_screen = (
        lax.all_gather(factor, "sub", axis=2, tiled=True),
        lax.all_gather(screen, "sub", axis=1, tiled=True),
    )
    whole = lax.all_gather(density, "row", axis=0, tiled=True)
    stacked = whole.reshape(nblocks, block_size, orbitals)
    panel = jnp.take(stacked, screen[0], axis=0).reshape(-1, orbitals)
    contracted = jnp.einsum(
        "ipk,kl->ipl", factor, panel, precision=precise, preferred_element_type=jnp.float32
    )
    tiled = contracted.reshape(block_size, aux_local, nblocks, block_size)
    zero_block = jnp.zeros((block_size, block_size), jnp.float32)
    rows_piece = lax.all_gather(full_rows[None], "row", axis=0, tiled=True)
    screen_piece = lax.all_gather(full_screen, "row", axis=0, tiled=True)
    count = rows_piece.shape[0]

    def single(member):
        offset, rows_one, screen_one = member
        return lax.cond(
            offset >= own_block, lambda: pair_block(tiled, rows_one, screen_one), lambda: zero_block
        )

    computed = lax.map(single, (jnp.arange(count, dtype=jnp.int32), rows_piece, screen_piece))
    updated = jnp.transpose(computed, (1, 0, 2))
    keep_mask = (jnp.arange(nblocks, dtype=jnp.int32) != own_block).astype(jnp.float32)
    received = lax.all_to_all(updated, "row", split_axis=1, concat_axis=1, tiled=True)
    mirrored = jnp.transpose(received, (2, 1, 0)) * keep_mask[None, :, None]
    partial_value = (updated + mirrored).reshape(block_size, orbitals)
    return lax.psum_scatter(partial_value, ("aux", "sub"), scatter_dimension=1, tiled=True)


def solution(mesh):
    sizes = tuple(mesh.shape[a] for a in ("row", "aux", "sub"))

    def body(factor, density, screen):
        nrow, naux, nsub = sizes
        block_size, orbitals = density.shape
        fits = (
            naux * nsub == 4
            and nsub == 2
            and nrow == 4
            and block_size == 64
            and orbitals == nrow * block_size
            and factor.shape[2] == 128
            and factor.shape[1] % (nrow * nsub * 2) == 0
        )
        if fits:
            return dealt_body(factor, density, screen)
        return gathered_body(factor, density, screen)

    return jax.shard_map(
        body,
        mesh=mesh,
        in_specs=(
            P(("dom", "row"), "aux", "sub"),
            P(("dom", "row"), None),
            P(("dom", "row"), "sub"),
        ),
        out_specs=P(("dom", "row"), ("aux", "sub")),
        check_vma=False,
    )
```
